32 devices in a mesh: win: 2 (over core), slab: 16 (over z, y, x).
Axes of the slice: x: 2, y: 2, z: 4, core: 2. Of those that a mesh axis runs over, the one named last changes fastest.
Arguments:
- states: float32 [2, 6, 32, 64, 256], P('win', None, 'slab'), may hold values from -6 to 6
- load_shape: bfloat16 [3, 32, 64, 256], P(None, 'slab'), may hold values from -6 to 6
- zone_ids: int32 [32, 64, 256], P('slab'), may hold values from 0 to 7
- zone_shear: float32 [8], replicated, may hold values from 0.3 to 1.2
- zone_lame: float32 [8], replicated, may hold values from 0.3 to 1.5
- amp_table: float32 [16], replicated, may hold values from 0.5 to 2
- cycle_index: int32 [16], replicated, may hold values from 0 to 15, each once
Outputs:
- new_ends: float32 [2, 6, 32, 64, 256], P('win', None, 'slab')
The draws below stay inside these ranges and needn't reach their ends.
Inputs may be any that keep to these rules, and one draw needn't show every extreme that they name: cycle_index holds each of 0 to 15 once.
All inputs are finite; a program needn't handle non-finite values.
Results may differ from the reference program's by a relative error of at most 0.0003.
Values sent between devices are 32-bit elements; how exact they have to be, the bound alone decides.
No kernel may reach another device: no remote copies, remote signals or barrier semaphores. Data moves between devices by JAX's collectives and lax.ppermute only.
A program may use at most 64 MiB of HBM per device.

```python
import math
import jax
import jax.numpy as jnp
from jax import lax

NY = 64
NX = 256
FINE = 4
COARSE = 2
ZONES = 8
CYCLES = 16
WINDOWS = 2
NZ = 32


def place_ends(entries, stream_key, least, largest):
    longest = entries.shape.index(max(entries.shape))
    spots = []
    for shift in (0, 1):
        where = [jax.random.randint(jax.random.fold_in(stream_key, axis), (), 0, length) for axis, length in enumerate(entries.shape)]
        where[longest] = (where[longest] + shift) % entries.shape[longest]
        spots.append(tuple(where))
    return entries.at[spots[0]].set(least).at[spots[1]].set(largest)


def steps_of(key, shape, cuts, smallest, high):
    gain = 1.0
    for dim, blocks in cuts:
        draws = jax.random.uniform(jax.random.fold_in(jax.random.fold_in(key, 6), dim), (blocks,), jnp.float32, smallest / len(cuts), high / len(cuts))
        gain = gain * jnp.repeat(jnp.exp(draws), shape[dim] // blocks).reshape((-1,) + (1,) * (len(shape) - 1 - dim))
    return gain


def centred(rng, shape, spread, limit, pieces=(), dtype=jnp.bfloat16):
    drawn = spread * jax.random.normal(rng, shape, jnp.float32)
    if pieces:
        drawn = drawn * steps_of(rng, shape, pieces, -0.22, 0.18)
    return jnp.clip(drawn, -limit, limit).astype(dtype)


def setup_inputs(seed: int = 0) -> dict:
    key_list = jax.random.split(jax.random.key(seed), 8)
    return {
        "states": centred(key_list[0], (WINDOWS, 6, NZ, NY, NX), 1.0, 6.0, ((0, 2), (2, 16)), jnp.float32),
        "load_shape": centred(key_list[1], (3, NZ, NY, NX), 1.0, 6.0, ((1, 16),)),
        "zone_ids": place_ends(jax.random.randint(key_list[2], (NZ, NY, NX), 0, ZONES), jax.random.fold_in(key_list[2], 1), 0, ZONES - 1).astype(jnp.int32),
        "zone_shear": jnp.clip(jnp.exp(jax.random.uniform(key_list[3], (ZONES,), jnp.float32, math.log(0.3), math.log(1.2))), 0.3, 1.2),
        "zone_lame": jnp.clip(jnp.exp(jax.random.uniform(key_list[4], (ZONES,), jnp.float32, math.log(0.3), math.log(1.5))), 0.3, 1.5),
        "amp_table": jnp.clip(jnp.exp(jax.random.uniform(key_list[5], (CYCLES,), jnp.float32, math.log(0.5), math.log(2.0))), 0.5, 2.0),
        "cycle_index": jax.random.permutation(key_list[6], CYCLES).astype(jnp.int32),
    }


DT_FINE = 0.18
DT_COARSE = 0.36
FACE_WEIGHT = 14.0 / 30.0
EDGE_WEIGHT = 3.0 / 30.0
CORNER_WEIGHT = 1.0 / 30.0


def combine(first_vec, second_vec, first_sign, second_sign):
    return tuple(first_sign * first_vec[i] + second_sign * second_vec[i] for i in range(3))


def acceleration(padded, stiff_shear, stiff_bulk, loading):
    layers = padded.shape[1] - 2
    stripes = padded.shape[2] - 2
    columns = padded.shape[3] - 2

    def shifted_by(offset):
        return padded[:, 1 + offset[0]:1 + offset[0] + layers, 1 + offset[1]:1 + offset[1] + stripes, 1 + offset[2]:1 + offset[2] + columns]

    centre = shifted_by((0, 0, 0))
    laplace = jnp.zeros_like(centre)
    for step_z in (-1, 0, 1):
        for step_y in (-1, 0, 1):
            for step_x in (-1, 0, 1):
                reach = abs(step_z) + abs(step_y) + abs(step_x)
                if reach > 0:
                    weight = (FACE_WEIGHT, EDGE_WEIGHT, CORNER_WEIGHT)[reach - 1]
                    laplace = laplace + weight * (shifted_by((step_z, step_y, step_x)) - centre)
    axis_units = ((0, 0, 1), (0, 1, 0), (1, 0, 0))
    coupled = []
    for component in range(3):
        own_unit = axis_units[component]
        along = shifted_by(own_unit)[component] + shifted_by(combine(own_unit, own_unit, -1, 0))[component] - 2.0 * centre[component]
        for other in range(3):
            if other != component:
                other_unit = axis_units[other]
                both_up = shifted_by(combine(own_unit, other_unit, 1, 1))[other]
                up_down = shifted_by(combine(own_unit, other_unit, 1, -1))[other]
                down_up = shifted_by(combine(own_unit, other_unit, -1, 1))[other]
                both_down = shifted_by(combine(own_unit, other_unit, -1, -1))[other]
                along = along + 0.25 * (both_up - up_down - down_up + both_down)
        coupled.append(along)
    coupling = jnp.stack(coupled)
    return stiff_shear * laplace + stiff_bulk * coupling + loading


def propagate(status, step_count, time_step, stiff_shear, stiff_bulk, loading, padder):
    def advance(turn_index, current):
        displaced = current[:3]
        velocity = current[3:]
        velocity = velocity + time_step * acceleration(padder(displaced), stiff_shear, stiff_bulk, loading)
        displaced = displaced + time_step * velocity
        return jnp.concatenate([displaced, velocity], axis=0)

    return lax.fori_loop(0, step_count, advance, status)


def pad_whole(displaced):
    return jnp.pad(displaced, ((0, 0), (1, 1), (1, 1), (1, 1)))


def reference(states, load_shape, zone_ids, zone_shear, zone_lame, amp_table, cycle_index):
    stiff_shear = zone_shear[zone_ids]
    stiff_bulk = zone_lame[zone_ids] + stiff_shear
    load_field = load_shape.astype(jnp.float32)
    results = []
    start_state = states[0]
    for window in range(WINDOWS):
        loading = amp_table[cycle_index[window]] * load_field
        fine_end = propagate(states[window], FINE, DT_FINE, stiff_shear, stiff_bulk, loading, pad_whole)
        coarse_old = propagate(states[window], COARSE, DT_COARSE, stiff_shear, stiff_bulk, loading, pad_whole)
        correction = fine_end - coarse_old
        advanced = propagate(start_state, COARSE, DT_COARSE, stiff_shear, stiff_bulk, loading, pad_whole) + correction
        results.append(advanced)
        start_state = advanced
    return jnp.stack(results)
```

```python
import jax
import jax.numpy as jnp
from jax import lax
from jax.sharding import PartitionSpec as P

FINE = 4
COARSE = 2


DT_FINE = 0.18
DT_COARSE = 0.36
FACE_WEIGHT = 14.0 / 30.0
EDGE_WEIGHT = 3.0 / 30.0
CORNER_WEIGHT = 1.0 / 30.0


def padded_2(block, sides, width):
    for axis, dim in sides:
        count = lax.axis_size(axis)
        forward = [(i, i + 1) for i in range(count - 1)]
        backward = [(target, source) for source, target in forward]
        low = lax.ppermute(
            lax.slice_in_dim(block, block.shape[dim] - width, None, axis=dim), axis, forward
        )
        high = lax.ppermute(lax.slice_in_dim(block, 0, width, axis=dim), axis, backward)
        block = jnp.concatenate([low, block, high], axis=dim)
    return block


def passed_along(block, axis, distance):
    devices = range(lax.axis_size(axis))
    route = [(i - distance, i) for i in devices if i - distance in devices]
    return lax.ppermute(block, axis, route)


def combine(first_vec, second_vec, first_sign, second_sign):
    return tuple((first_sign * first_vec[i] + second_sign * second_vec[i] for i in range(3)))


def acceleration(padded, stiff_shear, stiff_bulk, loading):
    layers = padded.shape[1] - 2
    stripes = padded.shape[2] - 2
    columns = padded.shape[3] - 2

    def shifted_by(offset):
        return padded[
            :,
            1 + offset[0] : 1 + offset[0] + layers,
            1 + offset[1] : 1 + offset[1] + stripes,
            1 + offset[2] : 1 + offset[2] + columns,
        ]

    centre = shifted_by((0, 0, 0))
    laplace = jnp.zeros_like(centre)
    for step_z in (-1, 0, 1):
        for step_y in (-1, 0, 1):
            for step_x in (-1, 0, 1):
                reach = abs(step_z) + abs(step_y) + abs(step_x)
                if reach > 0:
                    weight = (FACE_WEIGHT, EDGE_WEIGHT, CORNER_WEIGHT)[reach - 1]
                    laplace = laplace + weight * (shifted_by((step_z, step_y, step_x)) - centre)
    axis_units = ((0, 0, 1), (0, 1, 0), (1, 0, 0))
    coupled = []
    for component in range(3):
        own_unit = axis_units[component]
        along = (
            shifted_by(own_unit)[component]
            + shifted_by(combine(own_unit, own_unit, -1, 0))[component]
            - 2.0 * centre[component]
        )
        for other in range(3):
            if other != component:
                other_unit = axis_units[other]
                both_up = shifted_by(combine(own_unit, other_unit, 1, 1))[other]
                up_down = shifted_by(combine(own_unit, other_unit, 1, -1))[other]
                down_up = shifted_by(combine(own_unit, other_unit, -1, 1))[other]
                both_down = shifted_by(combine(own_unit, other_unit, -1, -1))[other]
                along = along + 0.25 * (both_up - up_down - down_up + both_down)
        coupled.append(along)
    coupling = jnp.stack(coupled)
    return stiff_shear * laplace + stiff_bulk * coupling + loading


def slab_rim(displaced):
    rimmed = padded_2(displaced, (("slab", 1),), 1)
    return jnp.pad(rimmed, ((0, 0), (0, 0), (1, 1), (1, 1)))


def propagate(status, step_count, time_step, stiff_shear, stiff_bulk, loading, padder):

    def advance(turn_index, current):
        displaced = current[:3]
        velocity = current[3:]
        velocity = velocity + time_step * acceleration(
            padder(displaced), stiff_shear, stiff_bulk, loading
        )
        displaced = displaced + time_step * velocity
        return jnp.concatenate([displaced, velocity], axis=0)

    return lax.fori_loop(0, step_count, advance, status)


def table_pick(table, position):
    return jnp.sum(
        jnp.where(
            jnp.arange(table.shape[0], dtype=jnp.int32) == position, table, jnp.zeros_like(table)
        )
    )


def shards(states, load_shape, zone_ids, zone_shear, zone_lame, amp_table, cycle_index):
    windows = lax.axis_size("win")
    window_index = lax.axis_index("win")
    zone_range = jnp.arange(zone_shear.shape[0], dtype=jnp.int32)
    matches = zone_ids[None] == zone_range[:, None, None, None]
    stiff_shear = jnp.sum(jnp.where(matches, zone_shear[:, None, None, None], 0.0), axis=0)
    lame_first = jnp.sum(jnp.where(matches, zone_lame[:, None, None, None], 0.0), axis=0)
    stiff_bulk = lame_first + stiff_shear
    load_field = load_shape.astype(jnp.float32)
    own_start = states[0]
    loading = table_pick(amp_table, table_pick(cycle_index, window_index)) * load_field
    fine_end = propagate(own_start, FINE, DT_FINE, stiff_shear, stiff_bulk, loading, slab_rim)
    first = window_index == 0
    silent = jnp.zeros_like(loading)

    def coarse(status):
        return propagate(status, COARSE, DT_COARSE, stiff_shear, stiff_bulk, silent, slab_rim)

    advanced = coarse(jnp.where(first, fine_end, own_start))
    correction = fine_end - jnp.where(first, jnp.zeros_like(advanced), advanced)

    def link(turn_index, current):
        return coarse(correction + passed_along(current, "win", 1))

    advanced = lax.fori_loop(0, windows - 2, link, advanced)
    new_end = correction + passed_along(advanced, "win", 1)
    return new_end[None]


def solution(mesh):
    placed = (
        P("win", None, "slab", None, None),
        P(None, "slab", None, None),
        P("slab", None, None),
        P(),
        P(),
        P(),
        P(),
    )
    return jax.shard_map(
        shards,
        mesh=mesh,
        in_specs=placed,
        out_specs=P("win", None, "slab", None, None),
        check_vma=False,
    )
```

```python
import functools

import jax
import jax.numpy as jnp
from jax import lax
from jax.experimental import pallas as pl
from jax.experimental.pallas import tpu as pltpu
from jax.sharding import PartitionSpec as P

FINE = 4
COARSE = 2


DT_FINE = 0.18
DT_COARSE = 0.36
FACE_WEIGHT = 14.0 / 30.0
EDGE_WEIGHT = 3.0 / 30.0
CORNER_WEIGHT = 1.0 / 30.0


def passed_along(block, axis, distance):
    devices = range(lax.axis_size(axis))
    route = [(i - distance, i) for i in devices if i - distance in devices]
    return lax.ppermute(block, axis, route)


def table_pick(table, position):
    return jnp.sum(
        jnp.where(
            jnp.arange(table.shape[0], dtype=jnp.int32) == position, table, jnp.zeros_like(table)
        )
    )


def padded_2(block, sides, width):
    for axis, dim in sides:
        count = lax.axis_size(axis)
        forward = [(i, i + 1) for i in range(count - 1)]
        backward = [(target, source) for source, target in forward]
        low = lax.ppermute(
            lax.slice_in_dim(block, block.shape[dim] - width, None, axis=dim), axis, forward
        )
        high = lax.ppermute(lax.slice_in_dim(block, 0, width, axis=dim), axis, backward)
        block = jnp.concatenate([low, block, high], axis=dim)
    return block


def combine(first_vec, second_vec, first_sign, second_sign):
    return tuple((first_sign * first_vec[i] + second_sign * second_vec[i] for i in range(3)))


def acceleration(padded, stiff_shear, stiff_bulk, loading):
    layers = padded.shape[1] - 2
    stripes = padded.shape[2] - 2
    columns = padded.shape[3] - 2

    def shifted_by(offset):
        return padded[
            :,
            1 + offset[0] : 1 + offset[0] + layers,
            1 + offset[1] : 1 + offset[1] + stripes,
            1 + offset[2] : 1 + offset[2] + columns,
        ]

    centre = shifted_by((0, 0, 0))
    laplace = jnp.zeros_like(centre)
    for step_z in (-1, 0, 1):
        for step_y in (-1, 0, 1):
            for step_x in (-1, 0, 1):
                reach = abs(step_z) + abs(step_y) + abs(step_x)
                if reach > 0:
                    weight = (FACE_WEIGHT, EDGE_WEIGHT, CORNER_WEIGHT)[reach - 1]
                    laplace = laplace + weight * (shifted_by((step_z, step_y, step_x)) - centre)
    axis_units = ((0, 0, 1), (0, 1, 0), (1, 0, 0))
    coupled = []
    for component in range(3):
        own_unit = axis_units[component]
        along = (
            shifted_by(own_unit)[component]
            + shifted_by(combine(own_unit, own_unit, -1, 0))[component]
            - 2.0 * centre[component]
        )
        for other in range(3):
            if other != component:
                other_unit = axis_units[other]
                both_up = shifted_by(combine(own_unit, other_unit, 1, 1))[other]
                up_down = shifted_by(combine(own_unit, other_unit, 1, -1))[other]
                down_up = shifted_by(combine(own_unit, other_unit, -1, 1))[other]
                both_down = shifted_by(combine(own_unit, other_unit, -1, -1))[other]
                along = along + 0.25 * (both_up - up_down - down_up + both_down)
        coupled.append(along)
    coupling = jnp.stack(coupled)
    return stiff_shear * laplace + stiff_bulk * coupling + loading


def slab_rim(displaced):
    rimmed = padded_2(displaced, (("slab", 1),), 1)
    return jnp.pad(rimmed, ((0, 0), (0, 0), (1, 1), (1, 1)))


def propagate(status, step_count, time_step, stiff_shear, stiff_bulk, loading, padder):

    def advance(turn_index, current):
        displaced = current[:3]
        velocity = current[3:]
        velocity = velocity + time_step * acceleration(
            padder(displaced), stiff_shear, stiff_bulk, loading
        )
        displaced = displaced + time_step * velocity
        return jnp.concatenate([displaced, velocity], axis=0)

    return lax.fori_loop(0, step_count, advance, status)


def shards_single(states, load_shape, zone_ids, zone_shear, zone_lame, amp_table, cycle_index):
    windows = lax.axis_size("win")
    window_index = lax.axis_index("win")
    zone_range = jnp.arange(zone_shear.shape[0], dtype=jnp.int32)
    matches = zone_ids[None] == zone_range[:, None, None, None]
    stiff_shear = jnp.sum(jnp.where(matches, zone_shear[:, None, None, None], 0.0), axis=0)
    lame_first = jnp.sum(jnp.where(matches, zone_lame[:, None, None, None], 0.0), axis=0)
    stiff_bulk = lame_first + stiff_shear
    load_field = load_shape.astype(jnp.float32)
    own_start = states[0]
    loading = table_pick(amp_table, table_pick(cycle_index, window_index)) * load_field
    fine_end = propagate(own_start, FINE, DT_FINE, stiff_shear, stiff_bulk, loading, slab_rim)
    first = window_index == 0
    silent = jnp.zeros_like(loading)

    def coarse(status):
        return propagate(status, COARSE, DT_COARSE, stiff_shear, stiff_bulk, silent, slab_rim)

    advanced = coarse(jnp.where(first, fine_end, own_start))
    correction = fine_end - jnp.where(first, jnp.zeros_like(advanced), advanced)

    def link(turn_index, current):
        return coarse(correction + passed_along(current, "win", 1))

    advanced = lax.fori_loop(0, windows - 2, link, advanced)
    new_end = correction + passed_along(advanced, "win", 1)
    return new_end[None]


class Inplane:
    def __init__(self, u):
        rows, columns = u[0].shape
        row = lax.broadcasted_iota(jnp.int32, (rows, columns), 0)
        column = lax.broadcasted_iota(jnp.int32, (rows, columns), 1)

        def shifted(f, axis, up):
            if up:
                edge = (row == rows - 1, column == columns - 1)[axis]
                return jnp.where(edge, 0.0, pltpu.roll(f, f.shape[axis] - 1, axis))
            edge = (row == 0, column == 0)[axis]
            return jnp.where(edge, 0.0, pltpu.roll(f, 1, axis))

        self.u = u
        self.shifted = shifted
        plus = [shifted(f, 1, True) for f in u]
        minus = [shifted(f, 1, False) for f in u]
        self.sum_x = [a + b for a, b in zip(plus, minus)]
        self.diff_x = [a - b for a, b in zip(plus, minus)]
        self.up_y = [None, shifted(u[1], 0, True), shifted(u[2], 0, True)]
        self.down_y = [None, shifted(u[1], 0, False), shifted(u[2], 0, False)]
        self.even = []
        for f, s in zip(u, self.sum_x):
            across = s + 3.0 * f
            square = shifted(across, 0, True) + shifted(across, 0, False) + 3.0 * across
            self.even.append((square + 5.0 * f) * (1.0 / 30.0))
        self.odd = [
            0.25 * self.diff_x[2],
            0.25 * (self.up_y[2] - self.down_y[2]),
            0.25 * (self.diff_x[0] + (self.up_y[1] - self.down_y[1])),
        ]

    def own(self):
        u, shifted = self.u, self.shifted
        up_x, down_x = shifted(u[0], 0, True), shifted(u[0], 0, False)
        sum_y = [up_x + down_x, self.up_y[1] + self.down_y[1], self.up_y[2] + self.down_y[2]]
        shear = [
            3.0 * e + (s + t) * (1.0 / 6.0) - (17.0 / 3.0) * f
            for e, s, t, f in zip(self.even, self.sum_x, sum_y, u)
        ]
        cross = [
            0.25 * (shifted(d, 0, True) - shifted(d, 0, False)) for d in self.diff_x[:2]
        ]
        bulk = [
            self.sum_x[0] - 2.0 * u[0] + cross[1],
            sum_y[1] - 2.0 * u[1] + cross[0],
            -2.0 * u[2],
        ]
        return shear, bulk


def towards(plane_sums, sign):
    odd = [sign * f for f in plane_sums[3:6]]
    return plane_sums[:3], [odd[0], odd[1], odd[2] + plane_sums[6]]


def sums_of(inplane):
    return (*inplane.even, *inplane.odd, inplane.u[2])


def partial_step(planes, velocity, shear, bulk, load, step):
    count = len(planes)
    outgoing = [sums_of(p) for p in planes]
    velocities, displaced = [], []
    for z, plane in enumerate(planes):
        even, other = plane.own()
        for neighbour, sign in ((z - 1, -1.0), (z + 1, 1.0)):
            if 0 <= neighbour < count:
                e, o = towards(outgoing[neighbour], sign)
                even = [a + b for a, b in zip(even, e)]
                other = [a + b for a, b in zip(other, o)]
        v = [
            velocity(c, z) + step * (shear(z) * even[c] + bulk(z) * other[c] + load(c, z))
            for c in range(3)
        ]
        velocities.append(v)
        displaced.append([plane.u[c] + step * v[c] for c in range(3)])
    return velocities, displaced, outgoing


def prepare(planes, velocity, shear, bulk, load, step, part_ref, up_ref, down_ref, rim_ref):
    count = len(planes)
    velocities, displaced, outgoing = partial_step(planes, velocity, shear, bulk, load, step)
    for z in range(count):
        for c in range(3):
            part_ref[c, z] = velocities[z][c]
    for c in range(3):
        down_ref[c] = planes[0].u[c]
        down_ref[3 + c] = displaced[0][c]
        up_ref[c] = planes[count - 1].u[c]
        up_ref[3 + c] = displaced[count - 1][c]
    for c in range(6):
        rim_ref[0, c] = outgoing[0][c]
        rim_ref[1, c] = outgoing[count - 1][c]


def zone_values(zone, shear_table, lame_table, offset):
    shear = jnp.zeros(zone.shape, jnp.float32)
    bulk = jnp.zeros(zone.shape, jnp.float32)
    for k in range(shear_table.shape[0]):
        hit = zone == k + offset
        shear = jnp.where(hit, shear_table[k], shear)
        bulk = jnp.where(hit, shear_table[k] + lame_table[k], bulk)
    return shear, bulk


def open_kernel(
    step, shear_table, lame_table, amp_ref, state, load_shape, zones,
    moduli, loading, part, up, down, rim,
):
    count = zones.shape[0]
    amplitude = amp_ref[0]
    for z in range(count):
        moduli[0, z], moduli[1, z] = zone_values(zones[z], shear_table, lame_table, 0)
        for c in range(3):
            loading[c, z] = amplitude * load_shape[c, z].astype(jnp.float32)
    planes = [Inplane([state[c, z] for c in range(3)]) for z in range(count)]
    prepare(
        planes,
        lambda c, z: state[3 + c, z],
        lambda z: moduli[0, z],
        lambda z: moduli[1, z],
        lambda c, z: loading[c, z],
        step, part, up, down, rim,
    )
    down[6] = (zones[0] + 1).astype(jnp.float32)
    up[6] = (zones[count - 1] + 1).astype(jnp.float32)


def two_steps(step, u0, part, rim, low, high, moduli, edges, load):
    count = moduli.shape[1]
    square = step * step
    sides = ((low, 0, 0, -1.0), (high, 1, count - 1, 1.0))
    velocities = [[part[c, z] for c in range(3)] for z in range(count)]
    outer = []
    for side, (got, edge, z, sign) in enumerate(sides):
        there = Inplane([got[c] for c in range(3)])
        even, odd = towards(sums_of(there), sign)
        for c in range(3):
            velocities[z][c] = velocities[z][c] + step * (
                moduli[0, z] * even[c] + moduli[1, z] * odd[c]
            )
        here = tuple(rim[side, c] for c in range(6)) + (u0[2, z],)
        even, odd = towards(here, -sign)
        outer.append(
            [
                got[3 + c] + square * (edges[2 * side] * even[c] + edges[2 * side + 1] * odd[c])
                for c in range(3)
            ]
        )
    planes = [
        Inplane([u0[c, z] + step * velocities[z][c] for c in range(3)]) for z in range(count)
    ]
    shear = lambda z: moduli[0, z]
    bulk = lambda z: moduli[1, z]
    ends, _, _ = partial_step(planes, lambda c, z: velocities[z][c], shear, bulk, load, step)
    for side, (got, edge, z, sign) in enumerate(sides):
        even, odd = towards(sums_of(Inplane(outer[side])), sign)
        for c in range(3):
            ends[z][c] = ends[z][c] + step * (shear(z) * even[c] + bulk(z) * odd[c])
    displaced = [[planes[z].u[c] + step * ends[z][c] for c in range(3)] for z in range(count)]
    return ends, displaced


def edge_moduli(zone_low, zone_high, shear_table, lame_table):
    return (
        *zone_values(zone_low, shear_table, lame_table, 1.0),
        *zone_values(zone_high, shear_table, lame_table, 1.0),
    )


def fine_kernel(
    step, last, shear_table, lame_table, first_ref, start, state, moduli, loading, part, rim,
    low, high, zone_low, zone_high, *outs,
):
    count = moduli.shape[1]
    edges = edge_moduli(zone_low[...], zone_high[...], shear_table, lame_table)
    ends, displaced = two_steps(
        step, state, part, rim, low, high, moduli, edges, lambda c, z: loading[c, z]
    )
    new_state, next_part, up, down, next_rim = outs[:5]
    for z in range(count):
        for c in range(3):
            new_state[c, z] = displaced[z][c]
            new_state[3 + c, z] = ends[z][c]
    if last:
        entry = outs[5]
        first = first_ref[0] == 1
        for z in range(count):
            for c in range(6):
                entry[c, z] = jnp.where(first, new_state[c, z], start[c, z])
        next_step, load = DT_COARSE, lambda c, z: 0.0
    else:
        entry = new_state
        next_step, load = step, lambda c, z: loading[c, z]
    planes = [Inplane([entry[c, z] for c in range(3)]) for z in range(count)]
    prepare(
        planes, lambda c, z: entry[3 + c, z], lambda z: moduli[0, z], lambda z: moduli[1, z],
        load, next_step, next_part, up, down, next_rim,
    )


def coarse_open_kernel(state, moduli, part, up, down, rim):
    count = moduli.shape[1]
    planes = [Inplane([state[c, z] for c in range(3)]) for z in range(count)]
    prepare(
        planes, lambda c, z: state[3 + c, z], lambda z: moduli[0, z], lambda z: moduli[1, z],
        lambda c, z: 0.0, DT_COARSE, part, up, down, rim,
    )


def coarse_kernel(
    shear_table, lame_table, state, moduli, part, rim, low, high, zone_low, zone_high, new_state
):
    edges = edge_moduli(zone_low[...], zone_high[...], shear_table, lame_table)
    ends, displaced = two_steps(
        DT_COARSE, state, part, rim, low, high, moduli, edges, lambda c, z: 0.0
    )
    for z in range(moduli.shape[1]):
        for c in range(3):
            new_state[c, z] = displaced[z][c]
            new_state[3 + c, z] = ends[z][c]


def called(kernel, outs, scalars, *operands):
    smem = pl.BlockSpec(memory_space=pltpu.SMEM)
    vmem = pl.BlockSpec(memory_space=pltpu.VMEM)
    return pl.pallas_call(
        kernel,
        out_shape=[jax.ShapeDtypeStruct(shape, jnp.float32) for shape in outs],
        in_specs=[smem] * len(scalars) + [vmem] * len(operands),
        out_specs=[vmem] * len(outs),
        compiler_params=pltpu.CompilerParams(vmem_limit_bytes=48 * 1024 * 1024),
    )(*scalars, *operands)


def exchanged(up, down):
    return passed_along(up, "slab", 1), passed_along(down, "slab", -1)


def shards(states, load_shape, zone_ids, zone_shear, zone_lame, amp_table, cycle_index):
    windows = lax.axis_size("win")
    window_index = lax.axis_index("win")
    first = window_index == 0
    first_flag = first.astype(jnp.int32).reshape(1)
    start = states[0]
    count, rows, columns = zone_ids.shape
    plane = (rows, columns)
    field, state = (3, count, *plane), (6, count, *plane)
    message, rims = (6, *plane), (2, 6, *plane)
    amplitude = amp_table[cycle_index[window_index]].reshape(1)
    tables = (zone_shear, zone_lame)

    moduli, loading, part, up, down, rim = called(
        functools.partial(open_kernel, DT_FINE),
        [(2, count, *plane), field, field, (7, *plane), (7, *plane), rims],
        (*tables, amplitude), start, load_shape, zone_ids,
    )
    low, high = exchanged(up, down)
    zones = low[6], high[6]
    current = start
    entry = None
    for turn in range(FINE // 2):
        last = turn == FINE // 2 - 1
        outs = [state, field, message, message, rims] + ([state] if last else [])
        current, part, up, down, rim, *entry = called(
            functools.partial(fine_kernel, DT_FINE, last), outs,
            (*tables, first_flag), start, current, moduli, loading, part, rim, low, high, *zones,
        )
        low, high = exchanged(up, down)
    fine_end = current

    def coarse_end(status, part, rim, low, high):
        return called(
            coarse_kernel, [state], tables, status, moduli, part, rim, low, high, *zones
        )[0]

    advanced = coarse_end(entry[0], part, rim, low, high)
    correction = fine_end - jnp.where(first, 0.0, advanced)
    for _ in range(windows - 2):
        status = correction + passed_along(advanced, "win", 1)
        part, up, down, rim = called(
            coarse_open_kernel, [field, message, message, rims], (), status, moduli
        )
        advanced = coarse_end(status, part, rim, *exchanged(up, down))
    everyone = lax.ppermute(advanced, "win", [(i, (i + 1) % windows) for i in range(windows)])
    new_end = correction + jnp.where(first, 0.0, everyone)
    return new_end[None]


def solution(mesh):
    placed = (
        P("win", None, "slab", None, None),
        P(None, "slab", None, None),
        P("slab", None, None),
        P(),
        P(),
        P(),
        P(),
    )

    def whole(states, *rest):
        planes = states.shape[2] // mesh.shape["slab"]
        return jax.shard_map(
            shards if planes >= 2 else shards_single,
            mesh=mesh,
            in_specs=placed,
            out_specs=P("win", None, "slab", None, None),
            check_vma=False,
        )(states, *rest)

    return whole
```

```python
import functools

import jax
import jax.numpy as jnp
from jax import lax
from jax.experimental import pallas as pl
from jax.experimental.pallas import tpu as pltpu
from jax.sharding import PartitionSpec as P

FINE = 4
COARSE = 2


DT_FINE = 0.18
DT_COARSE = 0.36


def passed_along(block, axis, distance):
    devices = range(lax.axis_size(axis))
    route = [(i - distance, i) for i in devices if i - distance in devices]
    return lax.ppermute(block, axis, route)


class Inplane:
    def __init__(self, u):
        rows, columns = u[0].shape
        row = lax.broadcasted_iota(jnp.int32, (rows, columns), 0)
        column = lax.broadcasted_iota(jnp.int32, (rows, columns), 1)

        def shifted(f, axis, up):
            if up:
                edge = (row == rows - 1, column == columns - 1)[axis]
                return jnp.where(edge, 0.0, pltpu.roll(f, f.shape[axis] - 1, axis))
            edge = (row == 0, column == 0)[axis]
            return jnp.where(edge, 0.0, pltpu.roll(f, 1, axis))

        self.u = u
        self.shifted = shifted
        plus = [shifted(f, 1, True) for f in u]
        minus = [shifted(f, 1, False) for f in u]
        self.sum_x = [a + b for a, b in zip(plus, minus)]
        self.diff_x = [a - b for a, b in zip(plus, minus)]
        self.up_y = [None, shifted(u[1], 0, True), shifted(u[2], 0, True)]
        self.down_y = [None, shifted(u[1], 0, False), shifted(u[2], 0, False)]
        self.even = []
        for f, s in zip(u, self.sum_x):
            across = s + 3.0 * f
            square = shifted(across, 0, True) + shifted(across, 0, False) + 3.0 * across
            self.even.append((square + 5.0 * f) * (1.0 / 30.0))
        self.odd = [
            0.25 * self.diff_x[2],
            0.25 * (self.up_y[2] - self.down_y[2]),
            0.25 * (self.diff_x[0] + (self.up_y[1] - self.down_y[1])),
        ]

    def own(self):
        u, shifted = self.u, self.shifted
        up_x, down_x = shifted(u[0], 0, True), shifted(u[0], 0, False)
        sum_y = [up_x + down_x, self.up_y[1] + self.down_y[1], self.up_y[2] + self.down_y[2]]
        shear = [
            3.0 * e + (s + t) * (1.0 / 6.0) - (17.0 / 3.0) * f
            for e, s, t, f in zip(self.even, self.sum_x, sum_y, u)
        ]
        cross = [
            0.25 * (shifted(d, 0, True) - shifted(d, 0, False)) for d in self.diff_x[:2]
        ]
        bulk = [
            self.sum_x[0] - 2.0 * u[0] + cross[1],
            sum_y[1] - 2.0 * u[1] + cross[0],
            -2.0 * u[2],
        ]
        return shear, bulk


def towards(plane_sums, sign):
    odd = [sign * f for f in plane_sums[3:6]]
    return plane_sums[:3], [odd[0], odd[1], odd[2] + plane_sums[6]]


def sums_of(inplane):
    return (*inplane.even, *inplane.odd, inplane.u[2])


def partial_step(planes, velocity, shear, bulk, load, step):
    count = len(planes)
    outgoing = [sums_of(p) for p in planes]
    velocities, displaced = [], []
    for z, plane in enumerate(planes):
        even, other = plane.own()
        for neighbour, sign in ((z - 1, -1.0), (z + 1, 1.0)):
            if 0 <= neighbour < count:
                e, o = towards(outgoing[neighbour], sign)
                even = [a + b for a, b in zip(even, e)]
                other = [a + b for a, b in zip(other, o)]
        v = [
            velocity(c, z) + step * (shear(z) * even[c] + bulk(z) * other[c] + load(c, z))
            for c in range(3)
        ]
        velocities.append(v)
        displaced.append([plane.u[c] + step * v[c] for c in range(3)])
    return velocities, displaced, outgoing


def prepare(planes, velocity, shear, bulk, load, step, part_ref, up_ref, down_ref, rim_ref):
    count = len(planes)
    velocities, displaced, outgoing = partial_step(planes, velocity, shear, bulk, load, step)
    for z in range(count):
        for c in range(3):
            part_ref[c, z] = velocities[z][c]
    for c in range(3):
        down_ref[c] = planes[0].u[c]
        down_ref[3 + c] = displaced[0][c]
        up_ref[c] = planes[count - 1].u[c]
        up_ref[3 + c] = displaced[count - 1][c]
    for c in range(6):
        rim_ref[0, c] = outgoing[0][c]
        rim_ref[1, c] = outgoing[count - 1][c]


def zone_values(zone, shear_table, lame_table, offset):
    shear = jnp.zeros(zone.shape, jnp.float32)
    bulk = jnp.zeros(zone.shape, jnp.float32)
    for k in range(shear_table.shape[0]):
        hit = zone == k + offset
        shear = jnp.where(hit, shear_table[k], shear)
        bulk = jnp.where(hit, shear_table[k] + lame_table[k], bulk)
    return shear, bulk


def open_kernel(
    step, state_hbm, load_hbm, zones_hbm, shear_hbm, lame_hbm, amp_hbm, cycle_hbm,
    moduli, loading, part, up, down, rim,
    state, load_shape, zones, shear_table, lame_table, amp_table, cycle_index, arrived,
):
    pairs = (
        (state_hbm.at[0], state), (cycle_hbm, cycle_index), (amp_hbm, amp_table),
        (shear_hbm, shear_table), (lame_hbm, lame_table), (zones_hbm, zones),
        (load_hbm, load_shape),
    )
    copies = [
        pltpu.make_async_copy(source, target, arrived.at[i])
        for i, (source, target) in enumerate(pairs)
    ]
    for copy in copies:
        copy.start()
    for copy in copies:
        copy.wait()
    count = zones.shape[0]
    amplitude = amp_table[cycle_index[lax.axis_index("win")]]
    for z in range(count):
        moduli[0, z], moduli[1, z] = zone_values(zones[z], shear_table, lame_table, 0)
        for c in range(3):
            loading[c, z] = amplitude * load_shape[c, z].astype(jnp.float32)
    planes = [Inplane([state[c, z] for c in range(3)]) for z in range(count)]
    prepare(
        planes,
        lambda c, z: state[3 + c, z],
        lambda z: moduli[0, z],
        lambda z: moduli[1, z],
        lambda c, z: loading[c, z],
        step, part, up, down, rim,
    )
    down[6] = (zones[0] + 1).astype(jnp.float32)
    up[6] = (zones[count - 1] + 1).astype(jnp.float32)


def two_steps(step, u0, part, rim, low, high, moduli, edges, load):
    count = moduli.shape[1]
    square = step * step
    sides = ((low, 0, 0, -1.0), (high, 1, count - 1, 1.0))
    velocities = [[part[c, z] for c in range(3)] for z in range(count)]
    outer = []
    for side, (got, edge, z, sign) in enumerate(sides):
        there = Inplane([got[c] for c in range(3)])
        even, odd = towards(sums_of(there), sign)
        for c in range(3):
            velocities[z][c] = velocities[z][c] + step * (
                moduli[0, z] * even[c] + moduli[1, z] * odd[c]
            )
        here = tuple(rim[side, c] for c in range(6)) + (u0[2, z],)
        even, odd = towards(here, -sign)
        outer.append(
            [
                got[3 + c] + square * (edges[2 * side] * even[c] + edges[2 * side + 1] * odd[c])
                for c in range(3)
            ]
        )
    planes = [
        Inplane([u0[c, z] + step * velocities[z][c] for c in range(3)]) for z in range(count)
    ]
    shear = lambda z: moduli[0, z]
    bulk = lambda z: moduli[1, z]
    ends, _, _ = partial_step(planes, lambda c, z: velocities[z][c], shear, bulk, load, step)
    for side, (got, edge, z, sign) in enumerate(sides):
        even, odd = towards(sums_of(Inplane(outer[side])), sign)
        for c in range(3):
            ends[z][c] = ends[z][c] + step * (shear(z) * even[c] + bulk(z) * odd[c])
    displaced = [[planes[z].u[c] + step * ends[z][c] for c in range(3)] for z in range(count)]
    return ends, displaced


def fine_kernel(
    step, turn, last, *refs
):
    if turn == 0:
        shear_table, lame_table, *refs = refs
    else:
        edges, *refs = refs
    start, state, moduli, loading, part, rim, low, high, *outs = refs
    if turn == 0:
        *outs, edges = outs
        edges[0], edges[1] = zone_values(low[6], shear_table, lame_table, 1.0)
        edges[2], edges[3] = zone_values(high[6], shear_table, lame_table, 1.0)
    count = moduli.shape[1]
    ends, displaced = two_steps(
        step, state, part, rim, low, high, moduli, edges, lambda c, z: loading[c, z]
    )
    new_state, next_part, up, down, next_rim = outs[:5]
    for z in range(count):
        for c in range(3):
            new_state[c, z] = displaced[z][c]
            new_state[3 + c, z] = ends[z][c]
    if last:
        entry = outs[5]
        first = lax.axis_index("win") == 0
        for z in range(count):
            for c in range(6):
                entry[c, z] = jnp.where(first, new_state[c, z], start[c, z])
        next_step, load = DT_COARSE, lambda c, z: 0.0
    else:
        entry = new_state
        next_step, load = step, lambda c, z: loading[c, z]
    planes = [Inplane([entry[c, z] for c in range(3)]) for z in range(count)]
    prepare(
        planes, lambda c, z: entry[3 + c, z], lambda z: moduli[0, z], lambda z: moduli[1, z],
        load, next_step, next_part, up, down, next_rim,
    )


def coarse_open_kernel(state, moduli, part, up, down, rim):
    count = moduli.shape[1]
    planes = [Inplane([state[c, z] for c in range(3)]) for z in range(count)]
    prepare(
        planes, lambda c, z: state[3 + c, z], lambda z: moduli[0, z], lambda z: moduli[1, z],
        lambda c, z: 0.0, DT_COARSE, part, up, down, rim,
    )


def coarse_kernel(edges, state, moduli, part, rim, low, high, new_state):
    ends, displaced = two_steps(
        DT_COARSE, state, part, rim, low, high, moduli, edges, lambda c, z: 0.0
    )
    for z in range(moduli.shape[1]):
        for c in range(3):
            new_state[c, z] = displaced[z][c]
            new_state[3 + c, z] = ends[z][c]


VMEM = pl.BlockSpec(memory_space=pltpu.VMEM)
SMEM = pl.BlockSpec(memory_space=pltpu.SMEM)
HBM = pl.BlockSpec(memory_space=pltpu.HBM)


def called(kernel, outs, *operands, scalars=0, specs=None, scratch=()):
    return pl.pallas_call(
        kernel,
        out_shape=[jax.ShapeDtypeStruct(shape, jnp.float32) for shape in outs],
        in_specs=specs or [SMEM] * scalars + [VMEM] * (len(operands) - scalars),
        out_specs=[VMEM] * len(outs),
        scratch_shapes=list(scratch),
        compiler_params=pltpu.CompilerParams(vmem_limit_bytes=16 * 1024 * 1024),
    )(*operands)


def exchanged(up, down):
    return passed_along(up, "slab", 1), passed_along(down, "slab", -1)


def shards(states, load_shape, zone_ids, zone_shear, zone_lame, amp_table, cycle_index):
    windows = lax.axis_size("win")
    first = lax.axis_index("win") == 0
    start = states[0]
    count, rows, columns = zone_ids.shape
    plane = (rows, columns)
    field, state = (3, count, *plane), (6, count, *plane)
    message, rims = (6, *plane), (2, 6, *plane)

    given = (states, load_shape, zone_ids, zone_shear, zone_lame, amp_table, cycle_index)
    moduli, loading, part, up, down, rim = called(
        functools.partial(open_kernel, DT_FINE),
        [(2, count, *plane), field, field, (7, *plane), (7, *plane), rims],
        *given,
        specs=[HBM] * len(given),
        scratch=[
            pltpu.VMEM(state, states.dtype),
            pltpu.VMEM(load_shape.shape, load_shape.dtype),
            pltpu.VMEM(zone_ids.shape, zone_ids.dtype),
            *[pltpu.SMEM(table.shape, table.dtype) for table in given[3:]],
            pltpu.SemaphoreType.DMA((len(given),)),
        ],
    )
    low, high = exchanged(up, down)
    current, edges = start, None
    for turn in range(FINE // 2):
        last = turn == FINE // 2 - 1
        outs = [state, field, message, message, rims]
        outs += ([state] if last else []) + ([(4, *plane)] if turn == 0 else [])
        tables = (zone_shear, zone_lame) if turn == 0 else (edges,)
        current, part, up, down, rim, *more = called(
            functools.partial(fine_kernel, DT_FINE, turn, last), outs,
            *tables, start, current, moduli, loading, part, rim, low, high,
            scalars=2 if turn == 0 else 0,
        )
        if turn == 0:
            edges = more.pop()
        low, high = exchanged(up, down)
    fine_end, entry = current, more[0]

    def coarse_end(status, part, rim, low, high):
        return called(coarse_kernel, [state], edges, status, moduli, part, rim, low, high)[0]

    advanced = coarse_end(entry, part, rim, low, high)
    correction = fine_end - jnp.where(first, 0.0, advanced)
    for _ in range(windows - 2):
        status = correction + passed_along(advanced, "win", 1)
        part, up, down, rim = called(
            coarse_open_kernel, [field, message, message, rims], status, moduli
        )
        advanced = coarse_end(status, part, rim, *exchanged(up, down))
    everyone = lax.ppermute(advanced, "win", [(i, (i + 1) % windows) for i in range(windows)])
    new_end = correction + jnp.where(first, 0.0, everyone)
    return new_end[None]


def solution(mesh):
    placed = (
        P("win", None, "slab", None, None),
        P(None, "slab", None, None),
        P("slab", None, None),
        P(),
        P(),
        P(),
        P(),
    )

    return jax.shard_map(
        shards,
        mesh=mesh,
        in_specs=placed,
        out_specs=P("win", None, "slab", None, None),
        check_vma=False,
    )
```

```python
import functools

import jax
import jax.numpy as jnp
from jax import lax
from jax.experimental import pallas as pl
from jax.experimental.pallas import tpu as pltpu
from jax.sharding import PartitionSpec as P

FINE = 4
DT_FINE = 0.18
DT_COARSE = 0.36


class Inplane:
    def __init__(self, u):
        rows, columns = u[0].shape
        row = lax.broadcasted_iota(jnp.int32, (rows, columns), 0)
        column = lax.broadcasted_iota(jnp.int32, (rows, columns), 1)

        def shifted(f, axis, up):
            if up:
                edge = (row == rows - 1, column == columns - 1)[axis]
                return jnp.where(edge, 0.0, pltpu.roll(f, f.shape[axis] - 1, axis))
            edge = (row == 0, column == 0)[axis]
            return jnp.where(edge, 0.0, pltpu.roll(f, 1, axis))

        self.u = u
        self.shifted = shifted
        plus = [shifted(f, 1, True) for f in u]
        minus = [shifted(f, 1, False) for f in u]
        self.sum_x = [a + b for a, b in zip(plus, minus)]
        self.diff_x = [a - b for a, b in zip(plus, minus)]
        self.up_y = [None, shifted(u[1], 0, True), shifted(u[2], 0, True)]
        self.down_y = [None, shifted(u[1], 0, False), shifted(u[2], 0, False)]
        self.even = []
        for f, s in zip(u, self.sum_x):
            across = s + 3.0 * f
            square = shifted(across, 0, True) + shifted(across, 0, False) + 3.0 * across
            self.even.append((square + 5.0 * f) * (1.0 / 30.0))
        self.odd = [
            0.25 * self.diff_x[2],
            0.25 * (self.up_y[2] - self.down_y[2]),
            0.25 * (self.diff_x[0] + (self.up_y[1] - self.down_y[1])),
        ]

    def own(self):
        u, shifted = self.u, self.shifted
        up_x, down_x = shifted(u[0], 0, True), shifted(u[0], 0, False)
        sum_y = [up_x + down_x, self.up_y[1] + self.down_y[1], self.up_y[2] + self.down_y[2]]
        shear = [
            3.0 * e + (s + t) * (1.0 / 6.0) - (17.0 / 3.0) * f
            for e, s, t, f in zip(self.even, self.sum_x, sum_y, u)
        ]
        cross = [
            0.25 * (shifted(d, 0, True) - shifted(d, 0, False)) for d in self.diff_x[:2]
        ]
        bulk = [
            self.sum_x[0] - 2.0 * u[0] + cross[1],
            sum_y[1] - 2.0 * u[1] + cross[0],
            -2.0 * u[2],
        ]
        return shear, bulk


def towards(plane_sums, sign):
    odd = [sign * f for f in plane_sums[3:6]]
    return plane_sums[:3], [odd[0], odd[1], odd[2] + plane_sums[6]]


def sums_of(inplane):
    return (*inplane.even, *inplane.odd, inplane.u[2])


def partial_step(planes, velocity, shear, bulk, load, step):
    count = len(planes)
    outgoing = [sums_of(p) for p in planes]
    velocities, displaced = [], []
    for z, plane in enumerate(planes):
        even, other = plane.own()
        for neighbour, sign in ((z - 1, -1.0), (z + 1, 1.0)):
            if 0 <= neighbour < count:
                e, o = towards(outgoing[neighbour], sign)
                even = [a + b for a, b in zip(even, e)]
                other = [a + b for a, b in zip(other, o)]
        v = [
            velocity(c, z) + step * (shear(z) * even[c] + bulk(z) * other[c] + load(c, z))
            for c in range(3)
        ]
        velocities.append(v)
        displaced.append([plane.u[c] + step * v[c] for c in range(3)])
    return velocities, displaced, outgoing


def prepare(planes, velocity, shear, bulk, load, step, part_ref, up_ref, down_ref, rim_ref):
    count = len(planes)
    velocities, displaced, outgoing = partial_step(planes, velocity, shear, bulk, load, step)
    for z in range(count):
        for c in range(3):
            part_ref[c, z] = velocities[z][c]
    for c in range(3):
        down_ref[c] = planes[0].u[c]
        down_ref[3 + c] = displaced[0][c]
        up_ref[c] = planes[count - 1].u[c]
        up_ref[3 + c] = displaced[count - 1][c]
    for c in range(6):
        rim_ref[0, c] = outgoing[0][c]
        rim_ref[1, c] = outgoing[count - 1][c]


def zone_values(zone, shear_table, lame_table, offset):
    shear = jnp.zeros(zone.shape, jnp.float32)
    bulk = jnp.zeros(zone.shape, jnp.float32)
    for k in range(shear_table.shape[0]):
        hit = zone == k + offset
        shear = jnp.where(hit, shear_table[k], shear)
        bulk = jnp.where(hit, shear_table[k] + lame_table[k], bulk)
    return shear, bulk


def open_kernel(
    step, state_hbm, load_hbm, zones_hbm, shear_hbm, lame_hbm, amp_hbm, cycle_hbm,
    moduli, loading, part, up, down, rim,
    state, load_shape, zones, shear_table, lame_table, amp_table, cycle_index, arrived,
):
    pairs = (
        (state_hbm.at[0], state), (cycle_hbm, cycle_index), (amp_hbm, amp_table),
        (shear_hbm, shear_table), (lame_hbm, lame_table), (zones_hbm, zones),
        (load_hbm, load_shape),
    )
    copies = [
        pltpu.make_async_copy(source, target, arrived.at[i])
        for i, (source, target) in enumerate(pairs)
    ]
    for copy in copies:
        copy.start()
    for copy in copies:
        copy.wait()
    count = zones.shape[0]
    amplitude = amp_table[cycle_index[lax.axis_index("win")]]
    for z in range(count):
        moduli[0, z], moduli[1, z] = zone_values(zones[z], shear_table, lame_table, 0)
        for c in range(3):
            loading[c, z] = amplitude * load_shape[c, z].astype(jnp.float32)
    planes = [Inplane([state[c, z] for c in range(3)]) for z in range(count)]
    prepare(
        planes,
        lambda c, z: state[3 + c, z],
        lambda z: moduli[0, z],
        lambda z: moduli[1, z],
        lambda c, z: loading[c, z],
        step, part, up, down, rim,
    )
    down[6] = (zones[0] + 1).astype(jnp.float32)
    up[6] = (zones[count - 1] + 1).astype(jnp.float32)


def two_steps(step, u0, part, rim, low, high, moduli, edges, load):
    count = moduli.shape[1]
    square = step * step
    sides = ((low, 0, 0, -1.0), (high, 1, count - 1, 1.0))
    velocities = [[part[c, z] for c in range(3)] for z in range(count)]
    outer = []
    for side, (got, edge, z, sign) in enumerate(sides):
        there = Inplane([got[c] for c in range(3)])
        even, odd = towards(sums_of(there), sign)
        for c in range(3):
            velocities[z][c] = velocities[z][c] + step * (
                moduli[0, z] * even[c] + moduli[1, z] * odd[c]
            )
        here = tuple(rim[side, c] for c in range(6)) + (u0[2, z],)
        even, odd = towards(here, -sign)
        outer.append(
            [
                got[3 + c] + square * (edges[2 * side] * even[c] + edges[2 * side + 1] * odd[c])
                for c in range(3)
            ]
        )
    planes = [
        Inplane([u0[c, z] + step * velocities[z][c] for c in range(3)]) for z in range(count)
    ]
    shear = lambda z: moduli[0, z]
    bulk = lambda z: moduli[1, z]
    ends, _, _ = partial_step(planes, lambda c, z: velocities[z][c], shear, bulk, load, step)
    for side, (got, edge, z, sign) in enumerate(sides):
        even, odd = towards(sums_of(Inplane(outer[side])), sign)
        for c in range(3):
            ends[z][c] = ends[z][c] + step * (shear(z) * even[c] + bulk(z) * odd[c])
    displaced = [[planes[z].u[c] + step * ends[z][c] for c in range(3)] for z in range(count)]
    return ends, displaced


def fine_kernel(step, turn, last, *refs):
    if turn == 0:
        shear_hbm, lame_hbm, *refs = refs
        *refs, shear_table, lame_table, arrived = refs
        copies = [
            pltpu.make_async_copy(shear_hbm, shear_table, arrived.at[0]),
            pltpu.make_async_copy(lame_hbm, lame_table, arrived.at[1]),
        ]
        for copy in copies:
            copy.start()
    else:
        edges, *refs = refs
    state, moduli, loading, part, rim, low, high, *outs = refs
    if turn == 0:
        *outs, edges = outs
        for copy in copies:
            copy.wait()
        edges[0], edges[1] = zone_values(low[6], shear_table, lame_table, 1.0)
        edges[2], edges[3] = zone_values(high[6], shear_table, lame_table, 1.0)
    count = moduli.shape[1]
    load = lambda c, z: loading[c, z]
    ends, displaced = two_steps(step, state, part, rim, low, high, moduli, edges, load)
    new_state = outs[0]
    for z in range(count):
        for c in range(3):
            new_state[c, z] = displaced[z][c]
            new_state[3 + c, z] = ends[z][c]
    if not last:
        planes = [Inplane(displaced[z]) for z in range(count)]
        prepare(
            planes, lambda c, z: ends[z][c], lambda z: moduli[0, z], lambda z: moduli[1, z],
            load, step, *outs[1:],
        )


def coarse_open_kernel(before, start, moduli, difference, part, up, down, rim):
    count = moduli.shape[1]
    for z in range(count):
        for c in range(6):
            difference[c, z] = before[c, z] - start[c, z]
    planes = [Inplane([difference[c, z] for c in range(3)]) for z in range(count)]
    prepare(
        planes, lambda c, z: difference[3 + c, z], lambda z: moduli[0, z],
        lambda z: moduli[1, z], lambda c, z: 0.0, DT_COARSE, part, up, down, rim,
    )


def coarse_kernel(edges, state, moduli, part, rim, low, high, fine_end, new_end):
    ends, displaced = two_steps(
        DT_COARSE, state, part, rim, low, high, moduli, edges, lambda c, z: 0.0
    )
    first = lax.axis_index("win") == 0
    for z in range(moduli.shape[1]):
        for c in range(3):
            new_end[c, z] = fine_end[c, z] + jnp.where(first, 0.0, displaced[z][c])
            new_end[3 + c, z] = fine_end[3 + c, z] + jnp.where(first, 0.0, ends[z][c])


VMEM = pl.BlockSpec(memory_space=pltpu.VMEM)
HBM = pl.BlockSpec(memory_space=pltpu.HBM)


def called(kernel, outs, *operands, in_specs=None, scratch=()):
    return pl.pallas_call(
        kernel,
        out_shape=[jax.ShapeDtypeStruct(shape, jnp.float32) for shape in outs],
        in_specs=in_specs or [VMEM] * len(operands),
        out_specs=[VMEM] * len(outs),
        scratch_shapes=list(scratch),
        compiler_params=pltpu.CompilerParams(vmem_limit_bytes=16 * 1024 * 1024),
    )(*operands)


def exchanged(up, down, first_window=0):
    windows, slabs = lax.axis_size("win"), lax.axis_size("slab")

    def passed(block, distance):
        route = [
            (n * slabs + i - distance, n * slabs + i)
            for n in range(first_window, windows)
            for i in range(slabs)
            if 0 <= i - distance < slabs
        ]
        return lax.ppermute(block, ("win", "slab"), route)

    return passed(up, 1), passed(down, -1)


def in_hbm(*arrays):
    return [pltpu.with_memory_space_constraint(a, pltpu.HBM) for a in arrays]


def shards(states, load_shape, zone_ids, zone_shear, zone_lame, amp_table, cycle_index):
    windows = lax.axis_size("win")
    start = states[0]
    count, rows, columns = zone_ids.shape
    plane = (rows, columns)
    field, state = (3, count, *plane), (6, count, *plane)
    message, rims = (6, *plane), (2, 6, *plane)

    given = (states, load_shape, zone_ids, zone_shear, zone_lame, amp_table, cycle_index)
    tables = [pltpu.SMEM(table.shape, table.dtype) for table in given[3:]]
    moduli, loading, part, up, down, rim = called(
        functools.partial(open_kernel, DT_FINE),
        [(2, count, *plane), field, field, (7, *plane), (7, *plane), rims],
        *in_hbm(*given),
        in_specs=[HBM] * len(given),
        scratch=[
            pltpu.VMEM(state, states.dtype),
            pltpu.VMEM(load_shape.shape, load_shape.dtype),
            pltpu.VMEM(zone_ids.shape, zone_ids.dtype),
            *tables,
            pltpu.SemaphoreType.DMA((len(given),)),
        ],
    )
    fine_end, edges = start, None
    for turn in range(FINE // 2):
        last = turn == FINE // 2 - 1
        low, high = exchanged(up, down)
        outs = [state] + ([] if last else [field, message, message, rims])
        operands = [fine_end, moduli, loading, part, rim, low, high]
        fine = functools.partial(fine_kernel, DT_FINE, turn, last)
        if turn == 0:
            fine_end, *more, edges = called(
                fine, [*outs, (4, *plane)], *in_hbm(zone_shear, zone_lame), *operands,
                in_specs=[HBM] * 2 + [VMEM] * len(operands),
                scratch=[*tables[:2], pltpu.SemaphoreType.DMA((2,))],
            )
        else:
            fine_end, *more = called(fine, outs, edges, *operands)
        if not last:
            part, up, down, rim = more

    new_end = fine_end
    for _ in range(windows - 1):
        before = lax.ppermute(new_end, "win", [(i, (i + 1) % windows) for i in range(windows)])
        difference, part, up, down, rim = called(
            coarse_open_kernel, [state, field, message, message, rims], before, start, moduli
        )
        low, high = exchanged(up, down, 1)
        new_end = called(
            coarse_kernel, [state], edges, difference, moduli, part, rim, low, high, fine_end
        )[0]
    return new_end[None]


def solution(mesh):
    placed = (
        P("win", None, "slab", None, None),
        P(None, "slab", None, None),
        P("slab", None, None),
        P(),
        P(),
        P(),
        P(),
    )

    return jax.shard_map(
        shards,
        mesh=mesh,
        in_specs=placed,
        out_specs=P("win", None, "slab", None, None),
        check_vma=False,
    )
```

```python
import functools

import jax
import jax.numpy as jnp
from jax import lax
from jax.experimental import pallas as pl
from jax.experimental.pallas import tpu as pltpu
from jax.sharding import PartitionSpec as P

FINE = 4
DT_FINE = 0.18
DT_COARSE = 0.36


class Inplane:
    def __init__(self, u):
        rows, columns = u[0].shape
        row = lax.broadcasted_iota(jnp.int32, (rows, columns), 0)
        column = lax.broadcasted_iota(jnp.int32, (rows, columns), 1)

        def shifted(f, axis, up):
            if up:
                edge = (row == rows - 1, column == columns - 1)[axis]
                return jnp.where(edge, 0.0, pltpu.roll(f, f.shape[axis] - 1, axis))
            edge = (row == 0, column == 0)[axis]
            return jnp.where(edge, 0.0, pltpu.roll(f, 1, axis))

        self.u = u
        self.shifted = shifted
        plus = [shifted(f, 1, True) for f in u]
        minus = [shifted(f, 1, False) for f in u]
        self.sum_x = [a + b for a, b in zip(plus, minus)]
        self.diff_x = [a - b for a, b in zip(plus, minus)]
        self.up_y = [None, shifted(u[1], 0, True), shifted(u[2], 0, True)]
        self.down_y = [None, shifted(u[1], 0, False), shifted(u[2], 0, False)]
        self.even = []
        for f, s in zip(u, self.sum_x):
            across = s + 3.0 * f
            square = shifted(across, 0, True) + shifted(across, 0, False) + 3.0 * across
            self.even.append((square + 5.0 * f) * (1.0 / 30.0))
        self.odd = [
            0.25 * self.diff_x[2],
            0.25 * (self.up_y[2] - self.down_y[2]),
            0.25 * (self.diff_x[0] + (self.up_y[1] - self.down_y[1])),
        ]

    def own(self):
        u, shifted = self.u, self.shifted
        up_x, down_x = shifted(u[0], 0, True), shifted(u[0], 0, False)
        sum_y = [up_x + down_x, self.up_y[1] + self.down_y[1], self.up_y[2] + self.down_y[2]]
        shear = [
            3.0 * e + (s + t) * (1.0 / 6.0) - (17.0 / 3.0) * f
            for e, s, t, f in zip(self.even, self.sum_x, sum_y, u)
        ]
        cross = [
            0.25 * (shifted(d, 0, True) - shifted(d, 0, False)) for d in self.diff_x[:2]
        ]
        bulk = [
            self.sum_x[0] - 2.0 * u[0] + cross[1],
            sum_y[1] - 2.0 * u[1] + cross[0],
            -2.0 * u[2],
        ]
        return shear, bulk


def towards(plane_sums, sign):
    odd = [sign * f for f in plane_sums[3:6]]
    return plane_sums[:3], [odd[0], odd[1], odd[2] + plane_sums[6]]


def sums_of(inplane):
    return (*inplane.even, *inplane.odd, inplane.u[2])


def partial_step(planes, velocity, shear, bulk, load, step):
    count = len(planes)
    outgoing = [sums_of(p) for p in planes]
    velocities, displaced = [], []
    for z, plane in enumerate(planes):
        even, other = plane.own()
        for neighbour, sign in ((z - 1, -1.0), (z + 1, 1.0)):
            if 0 <= neighbour < count:
                e, o = towards(outgoing[neighbour], sign)
                even = [a + b for a, b in zip(even, e)]
                other = [a + b for a, b in zip(other, o)]
        v = [
            velocity(c, z) + step * (shear(z) * even[c] + bulk(z) * other[c] + load(c, z))
            for c in range(3)
        ]
        velocities.append(v)
        displaced.append([plane.u[c] + step * v[c] for c in range(3)])
    return velocities, displaced, outgoing


def prepare(planes, velocity, shear, bulk, load, step, part_ref, up_ref, down_ref, rim_ref):
    count = len(planes)
    velocities, displaced, outgoing = partial_step(planes, velocity, shear, bulk, load, step)
    for z in range(count):
        for c in range(3):
            part_ref[c, z] = velocities[z][c]
    for c in range(3):
        down_ref[c] = planes[0].u[c]
        down_ref[3 + c] = displaced[0][c]
        up_ref[c] = planes[count - 1].u[c]
        up_ref[3 + c] = displaced[count - 1][c]
    for c in range(6):
        rim_ref[0, c] = outgoing[0][c]
        rim_ref[1, c] = outgoing[count - 1][c]


def zone_values(zone, shear_table, lame_table, offset):
    shear = jnp.zeros(zone.shape, jnp.float32)
    bulk = jnp.zeros(zone.shape, jnp.float32)
    for k in range(shear_table.shape[0]):
        hit = zone == k + offset
        shear = jnp.where(hit, shear_table[k], shear)
        bulk = jnp.where(hit, shear_table[k] + lame_table[k], bulk)
    return shear, bulk


def open_kernel(
    step, state_hbm, load_hbm, zones_hbm, shear_hbm, lame_hbm, amp_hbm, cycle_hbm,
    moduli, loading, part, up, down, rim,
    state, load_shape, zones, shear_table, lame_table, amp_table, cycle_index, arrived,
):
    pairs = (
        (state_hbm.at[0], state), (cycle_hbm, cycle_index), (amp_hbm, amp_table),
        (shear_hbm, shear_table), (lame_hbm, lame_table), (zones_hbm, zones),
        (load_hbm, load_shape),
    )
    copies = [
        pltpu.make_async_copy(source, target, arrived.at[i])
        for i, (source, target) in enumerate(pairs)
    ]
    for copy in copies:
        copy.start()
    for copy in copies:
        copy.wait()
    count = zones.shape[0]
    amplitude = amp_table[cycle_index[lax.axis_index("win")]]
    for z in range(count):
        moduli[0, z], moduli[1, z] = zone_values(zones[z], shear_table, lame_table, 0)
        for c in range(3):
            loading[c, z] = amplitude * load_shape[c, z].astype(jnp.float32)
    planes = [Inplane([state[c, z] for c in range(3)]) for z in range(count)]
    prepare(
        planes,
        lambda c, z: state[3 + c, z],
        lambda z: moduli[0, z],
        lambda z: moduli[1, z],
        lambda c, z: loading[c, z],
        step, part, up, down, rim,
    )
    down[6] = (zones[0] + 1).astype(jnp.float32)
    up[6] = (zones[count - 1] + 1).astype(jnp.float32)


def two_steps(step, u0, part, rim, low, high, moduli, edges, load):
    count = moduli.shape[1]
    square = step * step
    sides = ((low, 0, 0, -1.0), (high, 1, count - 1, 1.0))
    velocities = [[part[c, z] for c in range(3)] for z in range(count)]
    outer = []
    for side, (got, edge, z, sign) in enumerate(sides):
        there = Inplane([got[c] for c in range(3)])
        even, odd = towards(sums_of(there), sign)
        for c in range(3):
            velocities[z][c] = velocities[z][c] + step * (
                moduli[0, z] * even[c] + moduli[1, z] * odd[c]
            )
        here = tuple(rim[side, c] for c in range(6)) + (u0[2, z],)
        even, odd = towards(here, -sign)
        outer.append(
            [
                got[3 + c] + square * (edges[2 * side] * even[c] + edges[2 * side + 1] * odd[c])
                for c in range(3)
            ]
        )
    planes = [
        Inplane([u0[c, z] + step * velocities[z][c] for c in range(3)]) for z in range(count)
    ]
    shear = lambda z: moduli[0, z]
    bulk = lambda z: moduli[1, z]
    ends, _, _ = partial_step(planes, lambda c, z: velocities[z][c], shear, bulk, load, step)
    for side, (got, edge, z, sign) in enumerate(sides):
        even, odd = towards(sums_of(Inplane(outer[side])), sign)
        for c in range(3):
            ends[z][c] = ends[z][c] + step * (shear(z) * even[c] + bulk(z) * odd[c])
    displaced = [[planes[z].u[c] + step * ends[z][c] for c in range(3)] for z in range(count)]
    return ends, displaced


def released_kernel(up, down, token, later_up, later_down):
    @pl.when(lax.axis_index("win") != 0)
    def _():
        later_up[...] = up[...]
        later_down[...] = down[...]


def fine_kernel(step, turn, last, group, *refs):
    @pl.when((lax.axis_index("win") == 0) == (group == 0))
    def _():
        fine_pair(step, turn, last, *refs)


def fine_pair(step, turn, last, *refs):
    if turn == 0:
        shear_hbm, lame_hbm, *refs = refs
        *refs, shear_table, lame_table, arrived = refs
        copies = [
            pltpu.make_async_copy(shear_hbm, shear_table, arrived.at[0]),
            pltpu.make_async_copy(lame_hbm, lame_table, arrived.at[1]),
        ]
        for copy in copies:
            copy.start()
    else:
        edges, *refs = refs
    state, moduli, loading, part, rim, low, high, *outs = refs
    if turn == 0:
        *outs, edges = outs
        for copy in copies:
            copy.wait()
        edges[0], edges[1] = zone_values(low[6], shear_table, lame_table, 1.0)
        edges[2], edges[3] = zone_values(high[6], shear_table, lame_table, 1.0)
    count = moduli.shape[1]
    load = lambda c, z: loading[c, z]
    ends, displaced = two_steps(step, state, part, rim, low, high, moduli, edges, load)
    new_state = outs[0]
    for z in range(count):
        for c in range(3):
            new_state[c, z] = displaced[z][c]
            new_state[3 + c, z] = ends[z][c]
    if not last:
        planes = [Inplane(displaced[z]) for z in range(count)]
        prepare(
            planes, lambda c, z: ends[z][c], lambda z: moduli[0, z], lambda z: moduli[1, z],
            load, step, *outs[1:],
        )


def coarse_open_kernel(before, start, moduli, difference, part, up, down, rim):
    count = moduli.shape[1]
    for z in range(count):
        for c in range(6):
            difference[c, z] = before[c, z] - start[c, z]
    planes = [Inplane([difference[c, z] for c in range(3)]) for z in range(count)]
    prepare(
        planes, lambda c, z: difference[3 + c, z], lambda z: moduli[0, z],
        lambda z: moduli[1, z], lambda c, z: 0.0, DT_COARSE, part, up, down, rim,
    )


def coarse_kernel(edges, state, moduli, part, rim, low, high, before_end, fine_end, new_end):
    @pl.when(lax.axis_index("win") == 0)
    def _():
        new_end[...] = before_end[...]

    @pl.when(lax.axis_index("win") != 0)
    def _():
        ends, displaced = two_steps(
            DT_COARSE, state, part, rim, low, high, moduli, edges, lambda c, z: 0.0
        )
        for z in range(moduli.shape[1]):
            for c in range(3):
                new_end[c, z] = fine_end[c, z] + displaced[z][c]
                new_end[3 + c, z] = fine_end[3 + c, z] + ends[z][c]


VMEM = pl.BlockSpec(memory_space=pltpu.VMEM)
HBM = pl.BlockSpec(memory_space=pltpu.HBM)


def called(kernel, outs, *operands, in_specs=None, scratch=()):
    return pl.pallas_call(
        kernel,
        out_shape=[jax.ShapeDtypeStruct(shape, jnp.float32) for shape in outs],
        in_specs=in_specs or [VMEM] * len(operands),
        out_specs=[VMEM] * len(outs),
        scratch_shapes=list(scratch),
        compiler_params=pltpu.CompilerParams(vmem_limit_bytes=16 * 1024 * 1024),
    )(*operands)


def exchanged(up, down, group):
    windows, slabs = lax.axis_size("win"), lax.axis_size("slab")

    def passed(block, distance):
        route = [
            (n * slabs + i - distance, n * slabs + i)
            for n in (range(1, windows) if group else range(1))
            for i in range(slabs)
            if 0 <= i - distance < slabs
        ]
        return lax.ppermute(block, ("win", "slab"), route)

    return passed(up, 1), passed(down, -1)


def in_hbm(*arrays):
    return [pltpu.with_memory_space_constraint(a, pltpu.HBM) for a in arrays]


def shards(states, load_shape, zone_ids, zone_shear, zone_lame, amp_table, cycle_index):
    windows = lax.axis_size("win")
    start = states[0]
    count, rows, columns = zone_ids.shape
    plane = (rows, columns)
    field, state = (3, count, *plane), (6, count, *plane)
    message, rims = (6, *plane), (2, 6, *plane)

    given = (states, load_shape, zone_ids, zone_shear, zone_lame, amp_table, cycle_index)
    tables = [pltpu.SMEM(table.shape, table.dtype) for table in given[3:]]
    moduli, loading, part, up, down, rim = called(
        functools.partial(open_kernel, DT_FINE),
        [(2, count, *plane), field, field, (7, *plane), (7, *plane), rims],
        *in_hbm(*given),
        in_specs=[HBM] * len(given),
        scratch=[
            pltpu.VMEM(state, states.dtype),
            pltpu.VMEM(load_shape.shape, load_shape.dtype),
            pltpu.VMEM(zone_ids.shape, zone_ids.dtype),
            *tables,
            pltpu.SemaphoreType.DMA((len(given),)),
        ],
    )
    def fine(turn, group, edges, *operands):
        last = turn == FINE // 2 - 1
        outs = [state] + ([] if last else [field, message, message, rims])
        kernel = functools.partial(fine_kernel, DT_FINE, turn, last, group)
        if turn:
            return called(kernel, outs, edges, *operands)
        return called(
            kernel, [*outs, (4, *plane)], *in_hbm(zone_shear, zone_lame), *operands,
            in_specs=[HBM] * 2 + [VMEM] * len(operands),
            scratch=[*tables[:2], pltpu.SemaphoreType.DMA((2,))],
        )

    after = lax.optimization_barrier
    fixed = moduli, loading
    low, high = exchanged(up, down, 0)
    token = lax.ppermute(low[0, :8, :128], "win", [(n, n + 1) for n in range(windows - 1)])
    later_up, later_down = called(
        released_kernel, [(7, *plane), (7, *plane)], up, down, token
    )
    later_low, later_high = exchanged(later_up, later_down, 1)
    ends, parts, rim_of, edges = [start, start], [part, part], [rim, rim], [None, None]
    for turn in range(FINE // 2):
        last = turn == FINE // 2 - 1
        got = [(low, high), (later_low, later_high)]
        for group in (0, 1):
            if group == 0 or not last:
                ends[group], *more = fine(
                    turn, group, edges[group], ends[group], *fixed, parts[group], rim_of[group],
                    *got[group],
                )
                if turn == 0:
                    edges[group] = more.pop()
                if not last:
                    parts[group], up, down, rim_of[group] = more
                    if group == 0:
                        low, high = exchanged(up, down, 0)
                        later_low, later_high, _ = after((later_low, later_high, parts[0]))
                        got[1] = later_low, later_high
                    else:
                        later_low, later_high = exchanged(up, down, 1)
                        low, high, _ = after((low, high, parts[1]))

    new_end = ends[0]
    for link in range(windows - 1):
        before = lax.ppermute(new_end, "win", [(i, (i + 1) % windows) for i in range(windows)])
        difference, part, up, down, rim = called(
            coarse_open_kernel, [state, field, message, message, rims], before, start, moduli
        )
        low, high = exchanged(up, down, 1)
        if link == 0:
            later_low, later_high, _ = after((later_low, later_high, part))
            fine_end = fine(
                FINE // 2 - 1, 1, edges[1], ends[1], *fixed, parts[1], rim_of[1],
                later_low, later_high,
            )[0]
        new_end = called(
            coarse_kernel, [state],
            edges[1], difference, moduli, part, rim, low, high, ends[0], fine_end,
        )[0]
    return new_end[None]


def solution(mesh):
    placed = (
        P("win", None, "slab", None, None),
        P(None, "slab", None, None),
        P("slab", None, None),
        P(),
        P(),
        P(),
        P(),
    )

    return jax.shard_map(
        shards,
        mesh=mesh,
        in_specs=placed,
        out_specs=P("win", None, "slab", None, None),
        check_vma=False,
    )
```

```python
import functools

import jax
import jax.numpy as jnp
from jax import lax
from jax.experimental import pallas as pl
from jax.experimental.pallas import tpu as pltpu
from jax.sharding import PartitionSpec as P

FINE = 4
DT_FINE = 0.18
DT_COARSE = 0.36


class Inplane:
    def __init__(self, u):
        rows, columns = u[0].shape
        row = lax.broadcasted_iota(jnp.int32, (rows, columns), 0)
        column = lax.broadcasted_iota(jnp.int32, (rows, columns), 1)

        def shifted(f, axis, up):
            if up:
                edge = (row == rows - 1, column == columns - 1)[axis]
                return jnp.where(edge, 0.0, pltpu.roll(f, f.shape[axis] - 1, axis))
            edge = (row == 0, column == 0)[axis]
            return jnp.where(edge, 0.0, pltpu.roll(f, 1, axis))

        self.u = u
        self.shifted = shifted
        plus = [shifted(f, 1, True) for f in u]
        minus = [shifted(f, 1, False) for f in u]
        self.sum_x = [a + b for a, b in zip(plus, minus)]
        self.diff_x = [a - b for a, b in zip(plus, minus)]
        self.up_y = [None, shifted(u[1], 0, True), shifted(u[2], 0, True)]
        self.down_y = [None, shifted(u[1], 0, False), shifted(u[2], 0, False)]
        self.even = []
        for f, s in zip(u, self.sum_x):
            across = s + 3.0 * f
            square = shifted(across, 0, True) + shifted(across, 0, False) + 3.0 * across
            self.even.append((square + 5.0 * f) * (1.0 / 30.0))
        self.odd = [
            0.25 * self.diff_x[2],
            0.25 * (self.up_y[2] - self.down_y[2]),
            0.25 * (self.diff_x[0] + (self.up_y[1] - self.down_y[1])),
        ]

    def own(self):
        u, shifted = self.u, self.shifted
        up_x, down_x = shifted(u[0], 0, True), shifted(u[0], 0, False)
        sum_y = [up_x + down_x, self.up_y[1] + self.down_y[1], self.up_y[2] + self.down_y[2]]
        shear = [
            3.0 * e + (s + t) * (1.0 / 6.0) - (17.0 / 3.0) * f
            for e, s, t, f in zip(self.even, self.sum_x, sum_y, u)
        ]
        cross = [
            0.25 * (shifted(d, 0, True) - shifted(d, 0, False)) for d in self.diff_x[:2]
        ]
        bulk = [
            self.sum_x[0] - 2.0 * u[0] + cross[1],
            sum_y[1] - 2.0 * u[1] + cross[0],
            -2.0 * u[2],
        ]
        return shear, bulk


def towards(plane_sums, sign):
    odd = [sign * f for f in plane_sums[3:6]]
    return plane_sums[:3], [odd[0], odd[1], odd[2] + plane_sums[6]]


def sums_of(inplane):
    return (*inplane.even, *inplane.odd, inplane.u[2])


def partial_step(planes, velocity, shear, bulk, load, step):
    count = len(planes)
    outgoing = [sums_of(p) for p in planes]
    velocities, displaced = [], []
    for z, plane in enumerate(planes):
        even, other = plane.own()
        for neighbour, sign in ((z - 1, -1.0), (z + 1, 1.0)):
            if 0 <= neighbour < count:
                e, o = towards(outgoing[neighbour], sign)
                even = [a + b for a, b in zip(even, e)]
                other = [a + b for a, b in zip(other, o)]
        v = [
            velocity(c, z) + step * (shear(z) * even[c] + bulk(z) * other[c] + load(c, z))
            for c in range(3)
        ]
        velocities.append(v)
        displaced.append([plane.u[c] + step * v[c] for c in range(3)])
    return velocities, displaced, outgoing


def prepare(planes, velocity, shear, bulk, load, step, part_ref, up_ref, down_ref, rim_ref):
    count = len(planes)
    velocities, displaced, outgoing = partial_step(planes, velocity, shear, bulk, load, step)
    for z in range(count):
        for c in range(3):
            part_ref[c, z] = velocities[z][c]
    for c in range(3):
        down_ref[c] = planes[0].u[c]
        down_ref[3 + c] = displaced[0][c]
        up_ref[c] = planes[count - 1].u[c]
        up_ref[3 + c] = displaced[count - 1][c]
    for c in range(6):
        rim_ref[0, c] = outgoing[0][c]
        rim_ref[1, c] = outgoing[count - 1][c]


def zone_values(zone, shear_table, lame_table, offset):
    shear = jnp.zeros(zone.shape, jnp.float32)
    bulk = jnp.zeros(zone.shape, jnp.float32)
    for k in range(shear_table.shape[0]):
        hit = zone == k + offset
        shear = jnp.where(hit, shear_table[k], shear)
        bulk = jnp.where(hit, shear_table[k] + lame_table[k], bulk)
    return shear, bulk


def open_kernel(
    step, state_hbm, load_hbm, zones_hbm, shear_hbm, lame_hbm, amp_hbm, cycle_hbm,
    moduli, loading, part, up, down, rim, zone_up, zone_down,
    state, load_shape, zones, shear_table, lame_table, amp_table, cycle_index, arrived,
):
    pairs = (
        (state_hbm.at[0], state), (cycle_hbm, cycle_index), (amp_hbm, amp_table),
        (shear_hbm, shear_table), (lame_hbm, lame_table), (zones_hbm, zones),
        (load_hbm, load_shape),
    )
    copies = [
        pltpu.make_async_copy(source, target, arrived.at[i])
        for i, (source, target) in enumerate(pairs)
    ]
    for copy in copies:
        copy.start()
    for copy in copies:
        copy.wait()
    count = zones.shape[0]
    amplitude = amp_table[cycle_index[lax.axis_index("win")]]
    for z in range(count):
        moduli[0, z], moduli[1, z] = zone_values(zones[z], shear_table, lame_table, 0)
        for c in range(3):
            loading[c, z] = amplitude * load_shape[c, z].astype(jnp.float32)
    planes = [Inplane([state[c, z] for c in range(3)]) for z in range(count)]
    prepare(
        planes,
        lambda c, z: state[3 + c, z],
        lambda z: moduli[0, z],
        lambda z: moduli[1, z],
        lambda c, z: loading[c, z],
        step, part, up, down, rim,
    )
    zone_down[...] = (zones[0] + 1).astype(jnp.float32)
    zone_up[...] = (zones[count - 1] + 1).astype(jnp.float32)


def two_steps(step, u0, part, rim, low, high, moduli, edges, load):
    count = moduli.shape[1]
    square = step * step
    sides = ((low, 0, 0, -1.0), (high, 1, count - 1, 1.0))
    velocities = [[part[c, z] for c in range(3)] for z in range(count)]
    outer = []
    for side, (got, edge, z, sign) in enumerate(sides):
        there = Inplane([got[c] for c in range(3)])
        even, odd = towards(sums_of(there), sign)
        for c in range(3):
            velocities[z][c] = velocities[z][c] + step * (
                moduli[0, z] * even[c] + moduli[1, z] * odd[c]
            )
        here = tuple(rim[side, c] for c in range(6)) + (u0[2, z],)
        even, odd = towards(here, -sign)
        outer.append(
            [
                got[3 + c] + square * (edges[2 * side] * even[c] + edges[2 * side + 1] * odd[c])
                for c in range(3)
            ]
        )
    planes = [
        Inplane([u0[c, z] + step * velocities[z][c] for c in range(3)]) for z in range(count)
    ]
    shear = lambda z: moduli[0, z]
    bulk = lambda z: moduli[1, z]
    ends, _, _ = partial_step(planes, lambda c, z: velocities[z][c], shear, bulk, load, step)
    for side, (got, edge, z, sign) in enumerate(sides):
        even, odd = towards(sums_of(Inplane(outer[side])), sign)
        for c in range(3):
            ends[z][c] = ends[z][c] + step * (shear(z) * even[c] + bulk(z) * odd[c])
    displaced = [[planes[z].u[c] + step * ends[z][c] for c in range(3)] for z in range(count)]
    return ends, displaced


def edge_kernel(
    shear_hbm, lame_hbm, zone_low, zone_high, up, down, edges, later_up, later_down,
    shear_table, lame_table, arrived,
):
    @pl.when(lax.axis_index("win") != 0)
    def _():
        copies = [
            pltpu.make_async_copy(shear_hbm, shear_table, arrived.at[0]),
            pltpu.make_async_copy(lame_hbm, lame_table, arrived.at[1]),
        ]
        for copy in copies:
            copy.start()
        later_up[...] = up[...]
        later_down[...] = down[...]
        for copy in copies:
            copy.wait()
        edges[0], edges[1] = zone_values(zone_low[...], shear_table, lame_table, 1.0)
        edges[2], edges[3] = zone_values(zone_high[...], shear_table, lame_table, 1.0)


def fine_kernel(step, last, group, *refs):
    @pl.when((lax.axis_index("win") == 0) == (group == 0))
    def _():
        fine_pair(step, last, *refs)


def fine_pair(step, last, edges, state, moduli, loading, part, rim, low, high, *outs):
    count = moduli.shape[1]
    load = lambda c, z: loading[c, z]
    ends, displaced = two_steps(step, state, part, rim, low, high, moduli, edges, load)
    new_state = outs[0]
    for z in range(count):
        for c in range(3):
            new_state[c, z] = displaced[z][c]
            new_state[3 + c, z] = ends[z][c]
    if not last:
        planes = [Inplane(displaced[z]) for z in range(count)]
        prepare(
            planes, lambda c, z: ends[z][c], lambda z: moduli[0, z], lambda z: moduli[1, z],
            load, step, *outs[1:],
        )


def coarse_open_kernel(before, start, moduli, difference, part, up, down, rim):
    count = moduli.shape[1]
    for z in range(count):
        for c in range(6):
            difference[c, z] = before[c, z] - start[c, z]
    planes = [Inplane([difference[c, z] for c in range(3)]) for z in range(count)]
    prepare(
        planes, lambda c, z: difference[3 + c, z], lambda z: moduli[0, z],
        lambda z: moduli[1, z], lambda c, z: 0.0, DT_COARSE, part, up, down, rim,
    )


def coarse_kernel(edges, state, moduli, part, rim, low, high, before_end, fine_end, new_end):
    @pl.when(lax.axis_index("win") == 0)
    def _():
        new_end[...] = before_end[...]

    @pl.when(lax.axis_index("win") != 0)
    def _():
        ends, displaced = two_steps(
            DT_COARSE, state, part, rim, low, high, moduli, edges, lambda c, z: 0.0
        )
        for z in range(moduli.shape[1]):
            for c in range(3):
                new_end[c, z] = fine_end[c, z] + displaced[z][c]
                new_end[3 + c, z] = fine_end[3 + c, z] + ends[z][c]


VMEM = pl.BlockSpec(memory_space=pltpu.VMEM)
HBM = pl.BlockSpec(memory_space=pltpu.HBM)


def called(kernel, outs, *operands, in_specs=None, scratch=()):
    return pl.pallas_call(
        kernel,
        out_shape=[jax.ShapeDtypeStruct(shape, jnp.float32) for shape in outs],
        in_specs=in_specs or [VMEM] * len(operands),
        out_specs=[VMEM] * len(outs),
        scratch_shapes=list(scratch),
        compiler_params=pltpu.CompilerParams(vmem_limit_bytes=16 * 1024 * 1024),
    )(*operands)


def exchanged(up, down, group):
    windows, slabs = lax.axis_size("win"), lax.axis_size("slab")

    def passed(block, distance):
        route = [
            (n * slabs + i - distance, n * slabs + i)
            for n in (range(1, windows) if group else range(1))
            for i in range(slabs)
            if 0 <= i - distance < slabs
        ]
        return lax.ppermute(block, ("win", "slab"), route)

    return passed(up, 1), passed(down, -1)


def in_hbm(*arrays):
    return [pltpu.with_memory_space_constraint(a, pltpu.HBM) for a in arrays]


def shards(states, load_shape, zone_ids, zone_shear, zone_lame, amp_table, cycle_index):
    windows = lax.axis_size("win")
    start = states[0]
    count, rows, columns = zone_ids.shape
    plane = (rows, columns)
    field, state = (3, count, *plane), (6, count, *plane)
    message, rims = (6, *plane), (2, 6, *plane)

    given = (states, load_shape, zone_ids, zone_shear, zone_lame, amp_table, cycle_index)
    tables = [pltpu.SMEM(table.shape, table.dtype) for table in given[3:]]
    moduli, loading, part, up, down, rim, zone_up, zone_down = called(
        functools.partial(open_kernel, DT_FINE),
        [(2, count, *plane), field, field, message, message, rims, plane, plane],
        *in_hbm(*given),
        in_specs=[HBM] * len(given),
        scratch=[
            pltpu.VMEM(state, states.dtype),
            pltpu.VMEM(load_shape.shape, load_shape.dtype),
            pltpu.VMEM(zone_ids.shape, zone_ids.dtype),
            *tables,
            pltpu.SemaphoreType.DMA((len(given),)),
        ],
    )
    def fine(turn, group, *operands):
        last = turn == FINE // 2 - 1
        return called(
            functools.partial(fine_kernel, DT_FINE, last, group),
            [state] + ([] if last else [field, message, message, rims]),
            *operands,
        )

    after = lax.optimization_barrier
    fixed = moduli, loading
    low, high = exchanged(up, down, 0)
    edges, later_up, later_down = called(
        edge_kernel, [(4, *plane), message, message],
        *in_hbm(zone_shear, zone_lame), *exchanged(zone_up, zone_down, 1), up, down,
        in_specs=[HBM] * 2 + [VMEM] * 4,
        scratch=[*tables[:2], pltpu.SemaphoreType.DMA((2,))],
    )
    edges = lax.ppermute(edges, "win", [(1, 0)]), edges
    later_low, later_high = exchanged(later_up, later_down, 1)
    ends, parts, rim_of = [start, start], [part, part], [rim, rim]
    for turn in range(FINE // 2):
        last = turn == FINE // 2 - 1
        got = [(low, high), (later_low, later_high)]
        for group in (0, 1):
            if group == 0 or not last:
                ends[group], *more = fine(
                    turn, group, edges[group], ends[group], *fixed, parts[group], rim_of[group],
                    *got[group],
                )
                if not last:
                    parts[group], up, down, rim_of[group] = more
                    if group == 0:
                        low, high = exchanged(up, down, 0)
                        later_low, later_high, _ = after((later_low, later_high, parts[0]))
                        got[1] = later_low, later_high
                    else:
                        later_low, later_high = exchanged(up, down, 1)
                        low, high, _ = after((low, high, parts[1]))

    new_end = ends[0]
    for link in range(windows - 1):
        before = lax.ppermute(new_end, "win", [(n, n + 1) for n in range(windows - 1)])
        difference, part, up, down, rim = called(
            coarse_open_kernel, [state, field, message, message, rims], before, start, moduli
        )
        low, high = exchanged(up, down, 1)
        if link == 0:
            later_low, later_high, _ = after((later_low, later_high, part))
            fine_end = fine(
                FINE // 2 - 1, 1, edges[1], ends[1], *fixed, parts[1], rim_of[1],
                later_low, later_high,
            )[0]
        new_end = called(
            coarse_kernel, [state],
            edges[1], difference, moduli, part, rim, low, high, ends[0], fine_end,
        )[0]
    return new_end[None]


def solution(mesh):
    placed = (
        P("win", None, "slab", None, None),
        P(None, "slab", None, None),
        P("slab", None, None),
        P(),
        P(),
        P(),
        P(),
    )

    return jax.shard_map(
        shards,
        mesh=mesh,
        in_specs=placed,
        out_specs=P("win", None, "slab", None, None),
        check_vma=False,
    )
```

```python
import functools

import jax
import jax.numpy as jnp
from jax import lax
from jax.experimental import pallas as pl
from jax.experimental.pallas import tpu as pltpu
from jax.sharding import PartitionSpec as P

FINE = 4
DT_FINE = 0.18
DT_COARSE = 0.36


class Inplane:
    def __init__(self, u):
        rows, columns = u[0].shape
        tile, lanes = 8, columns // 2
        row = lax.broadcasted_iota(jnp.int32, (tile, columns), 0)
        lane = lax.broadcasted_iota(jnp.int32, (rows, lanes), 1)

        def shifted(f, axis, up):
            turned = pltpu.roll(f, f.shape[axis] - 1 if up else 1, axis)
            if axis == 0 and up:
                edge = jnp.where(row == tile - 1, 0.0, turned[rows - tile :])
                return jnp.concatenate([turned[: rows - tile], edge], axis=0)
            if axis == 0:
                edge = jnp.where(row == 0, 0.0, turned[:tile])
                return jnp.concatenate([edge, turned[tile:]], axis=0)
            if up:
                edge = jnp.where(lane == lanes - 1, 0.0, turned[:, lanes:])
                return jnp.concatenate([turned[:, :lanes], edge], axis=1)
            edge = jnp.where(lane == 0, 0.0, turned[:, :lanes])
            return jnp.concatenate([edge, turned[:, lanes:]], axis=1)

        self.u = u
        self.shifted = shifted
        plus = [shifted(f, 1, True) for f in u]
        minus = [shifted(f, 1, False) for f in u]
        self.sum_x = [a + b for a, b in zip(plus, minus)]
        self.diff_x = [a - b for a, b in zip(plus, minus)]
        self.up_y = [None, shifted(u[1], 0, True), shifted(u[2], 0, True)]
        self.down_y = [None, shifted(u[1], 0, False), shifted(u[2], 0, False)]
        self.even = []
        for f, s in zip(u, self.sum_x):
            across = s + 3.0 * f
            square = shifted(across, 0, True) + shifted(across, 0, False) + 3.0 * across
            self.even.append((square + 5.0 * f) * (1.0 / 30.0))
        self.odd = [
            0.25 * self.diff_x[2],
            0.25 * (self.up_y[2] - self.down_y[2]),
            0.25 * (self.diff_x[0] + (self.up_y[1] - self.down_y[1])),
        ]

    def own(self):
        u, shifted = self.u, self.shifted
        up_x, down_x = shifted(u[0], 0, True), shifted(u[0], 0, False)
        sum_y = [up_x + down_x, self.up_y[1] + self.down_y[1], self.up_y[2] + self.down_y[2]]
        shear = [
            3.0 * e + (s + t) * (1.0 / 6.0) - (17.0 / 3.0) * f
            for e, s, t, f in zip(self.even, self.sum_x, sum_y, u)
        ]
        cross = [
            0.25 * (shifted(d, 0, True) - shifted(d, 0, False)) for d in self.diff_x[:2]
        ]
        bulk = [
            self.sum_x[0] - 2.0 * u[0] + cross[1],
            sum_y[1] - 2.0 * u[1] + cross[0],
            -2.0 * u[2],
        ]
        return shear, bulk


def towards(plane_sums, sign):
    odd = [sign * f for f in plane_sums[3:6]]
    return plane_sums[:3], [odd[0], odd[1], odd[2] + plane_sums[6]]


def sums_of(inplane):
    return (*inplane.even, *inplane.odd, inplane.u[2])


def own_sums(planes):
    count = len(planes)
    outgoing = [sums_of(p) for p in planes]
    sums = []
    for z, plane in enumerate(planes):
        even, other = plane.own()
        for neighbour, sign in ((z - 1, -1.0), (z + 1, 1.0)):
            if 0 <= neighbour < count:
                e, o = towards(outgoing[neighbour], sign)
                even = [a + b for a, b in zip(even, e)]
                other = [a + b for a, b in zip(other, o)]
        sums.append((even, other))
    return sums, outgoing


def moved(sums, u, velocity, shear, bulk, load, step):
    even, other = sums
    v = [velocity[c] + step * (shear * even[c] + bulk * other[c] + load[c]) for c in range(3)]
    return v, [u[c] + step * v[c] for c in range(3)]


def prepare(sums, planes, velocity, shear, bulk, load, step, part_ref, up_ref, down_ref, rim_ref):
    sums, outgoing = sums
    last = len(planes) - 1
    for z, plane in enumerate(planes):
        v, displaced = moved(
            sums[z], plane.u, [velocity(c, z) for c in range(3)], shear(z), bulk(z),
            [load(c, z) for c in range(3)], step,
        )
        for c in range(3):
            part_ref[c, z] = v[c]
            for edge, ref in ((0, down_ref), (last, up_ref)):
                if z == edge:
                    ref[c] = plane.u[c]
                    ref[3 + c] = displaced[c]
    for c in range(6):
        rim_ref[0, c] = outgoing[0][c]
        rim_ref[1, c] = outgoing[last][c]


def zone_values(zone, shear_of, lame_of, zones, offset):
    shear = jnp.zeros(zone.shape, jnp.float32)
    bulk = jnp.zeros(zone.shape, jnp.float32)
    for k in range(zones):
        hit = zone == k + offset
        shear = jnp.where(hit, shear_of(k), shear)
        bulk = jnp.where(hit, shear_of(k) + lame_of(k), bulk)
    return shear, bulk


def open_kernel(
    step, state_hbm, load_hbm, zones_hbm, shear_hbm, lame_hbm, amp_hbm, cycle_hbm,
    moduli, loading, part, up, down, rim, zone_up, zone_down, zone_rows,
    state, load_shape, zones, shear_table, lame_table, amp_table, cycle_index, arrived,
):
    pairs = (
        (state_hbm.at[0, :3], state.at[:3]), (shear_hbm, shear_table), (lame_hbm, lame_table),
        (zones_hbm, zones), (cycle_hbm, cycle_index), (amp_hbm, amp_table),
        (load_hbm, load_shape), (state_hbm.at[0, 3:], state.at[3:]),
    )
    copies = [
        pltpu.make_async_copy(source, target, arrived.at[i])
        for i, (source, target) in enumerate(pairs)
    ]
    for copy in copies:
        copy.start()
    copies[0].wait()
    count, _, columns = zones.shape
    planes = [Inplane([state[c, z] for c in range(3)]) for z in range(count)]
    sums = own_sums(planes)
    for copy in copies[1:]:
        copy.wait()
    kinds = shear_table.shape[0]
    for z in range(count):
        moduli[0, z], moduli[1, z] = zone_values(
            zones[z], lambda k: shear_table[k], lambda k: lame_table[k], kinds, 0
        )
    amplitude = amp_table[cycle_index[lax.axis_index("win")]]
    for z in range(count):
        for c in range(3):
            loading[c, z] = amplitude * load_shape[c, z].astype(jnp.float32)
    prepare(
        sums, planes,
        lambda c, z: state[3 + c, z],
        lambda z: moduli[0, z],
        lambda z: moduli[1, z],
        lambda c, z: loading[c, z],
        step, part, up, down, rim,
    )
    zone_down[...] = (zones[0] + 1).astype(jnp.float32)
    zone_up[...] = (zones[count - 1] + 1).astype(jnp.float32)
    for k in range(kinds):
        zone_rows[k] = jnp.full((1, columns), shear_table[k], jnp.float32)
        zone_rows[kinds + k] = jnp.full((1, columns), lame_table[k], jnp.float32)


def two_steps(step, u0, part, rim, low, high, moduli, edges, load):
    count = moduli.shape[1]
    square = step * step
    sides = ((low, 0, 0, -1.0), (high, 1, count - 1, 1.0))
    velocities = [[part[c, z] for c in range(3)] for z in range(count)]
    outer = []
    for side, (got, edge, z, sign) in enumerate(sides):
        there = Inplane([got[c] for c in range(3)])
        even, odd = towards(sums_of(there), sign)
        for c in range(3):
            velocities[z][c] = velocities[z][c] + step * (
                moduli[0, z] * even[c] + moduli[1, z] * odd[c]
            )
        here = tuple(rim[side, c] for c in range(6)) + (u0[2, z],)
        even, odd = towards(here, -sign)
        outer.append(
            [
                got[3 + c] + square * (edges[2 * side] * even[c] + edges[2 * side + 1] * odd[c])
                for c in range(3)
            ]
        )
    planes = [
        Inplane([u0[c, z] + step * velocities[z][c] for c in range(3)]) for z in range(count)
    ]
    sums, _ = own_sums(planes)
    for side, (got, edge, z, sign) in enumerate(sides):
        part_of = towards(sums_of(Inplane(outer[side])), sign)
        sums[z] = tuple([a + b for a, b in zip(x, y)] for x, y in zip(sums[z], part_of))
    return [
        moved(
            sums[z], planes[z].u, velocities[z], moduli[0, z], moduli[1, z],
            [load(c, z) for c in range(3)], step,
        )
        for z in range(count)
    ]


def edge_kernel(zone_low, zone_high, zone_rows, up, down, edges, later_up, later_down):
    @pl.when(lax.axis_index("win") != 0)
    def _():
        kinds = zone_rows.shape[0] // 2
        for i, zone in enumerate((zone_low, zone_high)):
            edges[2 * i], edges[2 * i + 1] = zone_values(
                zone[...], lambda k: zone_rows[k], lambda k: zone_rows[kinds + k], kinds, 1.0
            )
        later_up[...] = up[...]
        later_down[...] = down[...]


def stored(state, ends):
    for z, (v, u) in enumerate(ends):
        for c in range(3):
            state[c, z] = u[c]
            state[3 + c, z] = v[c]


def fine_kernel(step, last, group, *refs):
    @pl.when((lax.axis_index("win") == 0) == (group == 0))
    def _():
        fine_pair(step, last, *refs)


def fine_pair(step, last, edges, state, moduli, loading, part, rim, low, high, *outs):
    load = lambda c, z: loading[c, z]
    ends = two_steps(step, state, part, rim, low, high, moduli, edges, load)
    stored(outs[0], ends)
    if not last:
        planes = [Inplane(u) for _, u in ends]
        prepare(
            own_sums(planes), planes, lambda c, z: ends[z][0][c], lambda z: moduli[0, z],
            lambda z: moduli[1, z], load, step, *outs[1:],
        )


def coarse_open_kernel(before, start, moduli, difference, part, up, down, rim):
    count = moduli.shape[1]
    planes = []
    for z in range(count):
        for c in range(6):
            difference[c, z] = before[c, z] - start[c, z]
        planes.append(Inplane([difference[c, z] for c in range(3)]))
    prepare(
        own_sums(planes), planes, lambda c, z: difference[3 + c, z], lambda z: moduli[0, z],
        lambda z: moduli[1, z], lambda c, z: 0.0, DT_COARSE, part, up, down, rim,
    )


def coarse_kernel(
    edges, state, moduli, part, rim, low, high, before_end, fine_end, new_end, end, left
):
    copies = [
        pltpu.make_async_copy(end.at[:, z], new_end.at[:, z], left.at[z])
        for z in range(moduli.shape[1])
    ]

    @pl.when(lax.axis_index("win") == 0)
    def _():
        end[...] = before_end[...]
        for copy in copies:
            copy.start()

    @pl.when(lax.axis_index("win") != 0)
    def _():
        ends = two_steps(
            DT_COARSE, state, part, rim, low, high, moduli, edges, lambda c, z: 0.0
        )
        for z, (v, u) in enumerate(ends):
            for c in range(3):
                end[c, z] = fine_end[c, z] + u[c]
                end[3 + c, z] = fine_end[3 + c, z] + v[c]
            copies[z].start()

    for copy in copies:
        copy.wait()


VMEM = pl.BlockSpec(memory_space=pltpu.VMEM)
HBM = pl.BlockSpec(memory_space=pltpu.HBM)


def called(kernel, outs, *operands, in_specs=None, out_specs=None, scratch=()):
    return pl.pallas_call(
        kernel,
        out_shape=[jax.ShapeDtypeStruct(shape, jnp.float32) for shape in outs],
        in_specs=in_specs or [VMEM] * len(operands),
        out_specs=out_specs or [VMEM] * len(outs),
        scratch_shapes=list(scratch),
        compiler_params=pltpu.CompilerParams(vmem_limit_bytes=16 * 1024 * 1024),
    )(*operands)


def exchanged(up, down, group):
    windows, slabs = lax.axis_size("win"), lax.axis_size("slab")

    def passed(block, distance):
        route = [
            (n * slabs + i - distance, n * slabs + i)
            for n in (range(1, windows) if group else range(1))
            for i in range(slabs)
            if 0 <= i - distance < slabs
        ]
        return lax.ppermute(block, ("win", "slab"), route)

    return passed(up, 1), passed(down, -1)


def in_hbm(*arrays):
    return [pltpu.with_memory_space_constraint(a, pltpu.HBM) for a in arrays]


def shards(states, load_shape, zone_ids, zone_shear, zone_lame, amp_table, cycle_index):
    windows = lax.axis_size("win")
    start = states[0]
    count, rows, columns = zone_ids.shape
    plane = (rows, columns)
    field, state = (3, count, *plane), (6, count, *plane)
    message, rims = (6, *plane), (2, 6, *plane)

    given = (states, load_shape, zone_ids, zone_shear, zone_lame, amp_table, cycle_index)
    tables = [pltpu.SMEM(table.shape, table.dtype) for table in given[3:]]
    zone_rows = (2 * zone_shear.shape[0], 1, columns)
    moduli, loading, part, up, down, rim, zone_up, zone_down, zone_rows = called(
        functools.partial(open_kernel, DT_FINE),
        [(2, count, *plane), field, field, message, message, rims, plane, plane, zone_rows],
        *in_hbm(*given),
        in_specs=[HBM] * len(given),
        scratch=[
            pltpu.VMEM(state, states.dtype),
            pltpu.VMEM(load_shape.shape, load_shape.dtype),
            pltpu.VMEM(zone_ids.shape, zone_ids.dtype),
            *tables,
            pltpu.SemaphoreType.DMA((len(given) + 1,)),
        ],
    )
    def fine(turn, group, *operands):
        last = turn == FINE // 2 - 1
        return called(
            functools.partial(fine_kernel, DT_FINE, last, group),
            [state] + ([] if last else [field, message, message, rims]),
            *operands,
        )

    after = lax.optimization_barrier
    fixed = moduli, loading
    low, high = exchanged(up, down, 0)
    edges, later_up, later_down = called(
        edge_kernel, [(4, *plane), message, message],
        *exchanged(zone_up, zone_down, 1), zone_rows, up, down,
    )
    edges = lax.ppermute(edges, "win", [(1, 0)]), edges
    later_low, later_high = exchanged(later_up, later_down, 1)
    ends, parts, rim_of = [start, start], [part, part], [rim, rim]
    for turn in range(FINE // 2):
        last = turn == FINE // 2 - 1
        got = [(low, high), (later_low, later_high)]
        for group in (0, 1):
            if group == 0 or not last:
                ends[group], *more = fine(
                    turn, group, edges[group], ends[group], *fixed, parts[group], rim_of[group],
                    *got[group],
                )
                if not last:
                    parts[group], up, down, rim_of[group] = more
                    if group == 0:
                        low, high = exchanged(up, down, 0)
                        later_low, later_high, _ = after((later_low, later_high, parts[0]))
                        got[1] = later_low, later_high
                    else:
                        later_low, later_high = exchanged(up, down, 1)
                        low, high, _ = after((low, high, parts[1]))

    new_end = ends[0]
    for link in range(windows - 1):
        before = lax.ppermute(new_end, "win", [(n, n + 1) for n in range(windows - 1)])
        difference, part, up, down, rim = called(
            coarse_open_kernel, [state, field, message, message, rims], before, start, moduli
        )
        low, high = exchanged(up, down, 1)
        if link == 0:
            later_low, later_high, _ = after((later_low, later_high, part))
            fine_end = fine(
                FINE // 2 - 1, 1, edges[1], ends[1], *fixed, parts[1], rim_of[1],
                later_low, later_high,
            )[0]
        new_end = called(
            coarse_kernel, [state],
            edges[1], difference, moduli, part, rim, low, high, ends[0], fine_end,
            out_specs=[HBM],
            scratch=[pltpu.VMEM(state, jnp.float32), pltpu.SemaphoreType.DMA((count,))],
        )[0]
    return new_end[None]


def solution(mesh):
    placed = (
        P("win", None, "slab", None, None),
        P(None, "slab", None, None),
        P("slab", None, None),
        P(),
        P(),
        P(),
        P(),
    )

    return jax.shard_map(
        shards,
        mesh=mesh,
        in_specs=placed,
        out_specs=P("win", None, "slab", None, None),
        check_vma=False,
    )
```

```python
import functools

import jax
import jax.numpy as jnp
from jax import lax
from jax.experimental import pallas as pl
from jax.experimental.pallas import tpu as pltpu
from jax.sharding import PartitionSpec as P

FINE = 4
DT_FINE = 0.18
DT_COARSE = 0.36


class Inplane:
    def __init__(self, u):
        rows, columns = u[0].shape
        tile, lanes = 8, columns // 2
        row = lax.broadcasted_iota(jnp.int32, (tile, columns), 0)
        lane = lax.broadcasted_iota(jnp.int32, (rows, lanes), 1)

        def shifted(f, axis, up):
            turned = pltpu.roll(f, f.shape[axis] - 1 if up else 1, axis)
            if axis == 0 and up:
                edge = jnp.where(row == tile - 1, 0.0, turned[rows - tile :])
                return jnp.concatenate([turned[: rows - tile], edge], axis=0)
            if axis == 0:
                edge = jnp.where(row == 0, 0.0, turned[:tile])
                return jnp.concatenate([edge, turned[tile:]], axis=0)
            if up:
                edge = jnp.where(lane == lanes - 1, 0.0, turned[:, lanes:])
                return jnp.concatenate([turned[:, :lanes], edge], axis=1)
            edge = jnp.where(lane == 0, 0.0, turned[:, :lanes])
            return jnp.concatenate([edge, turned[:, lanes:]], axis=1)

        self.u = u
        self.shifted = shifted
        plus = [shifted(f, 1, True) for f in u]
        minus = [shifted(f, 1, False) for f in u]
        self.sum_x = [a + b for a, b in zip(plus, minus)]
        self.diff_x = [a - b for a, b in zip(plus, minus)]
        self.up_y = [None, shifted(u[1], 0, True), shifted(u[2], 0, True)]
        self.down_y = [None, shifted(u[1], 0, False), shifted(u[2], 0, False)]
        self.even = []
        for f, s in zip(u, self.sum_x):
            across = s + 3.0 * f
            square = shifted(across, 0, True) + shifted(across, 0, False) + 3.0 * across
            self.even.append((square + 5.0 * f) * (1.0 / 30.0))
        self.odd = [
            0.25 * self.diff_x[2],
            0.25 * (self.up_y[2] - self.down_y[2]),
            0.25 * (self.diff_x[0] + (self.up_y[1] - self.down_y[1])),
        ]

    def own(self):
        u, shifted = self.u, self.shifted
        up_x, down_x = shifted(u[0], 0, True), shifted(u[0], 0, False)
        sum_y = [up_x + down_x, self.up_y[1] + self.down_y[1], self.up_y[2] + self.down_y[2]]
        shear = [
            3.0 * e + (s + t) * (1.0 / 6.0) - (17.0 / 3.0) * f
            for e, s, t, f in zip(self.even, self.sum_x, sum_y, u)
        ]
        cross = [
            0.25 * (shifted(d, 0, True) - shifted(d, 0, False)) for d in self.diff_x[:2]
        ]
        bulk = [
            self.sum_x[0] - 2.0 * u[0] + cross[1],
            sum_y[1] - 2.0 * u[1] + cross[0],
            -2.0 * u[2],
        ]
        return shear, bulk


def towards(plane_sums, sign):
    odd = [sign * f for f in plane_sums[3:6]]
    return plane_sums[:3], [odd[0], odd[1], odd[2] + plane_sums[6]]


def sums_of(inplane):
    return (*inplane.even, *inplane.odd, inplane.u[2])


def own_sums(planes):
    count = len(planes)
    outgoing = [sums_of(p) for p in planes]
    sums = []
    for z, plane in enumerate(planes):
        even, other = plane.own()
        for neighbour, sign in ((z - 1, -1.0), (z + 1, 1.0)):
            if 0 <= neighbour < count:
                e, o = towards(outgoing[neighbour], sign)
                even = [a + b for a, b in zip(even, e)]
                other = [a + b for a, b in zip(other, o)]
        sums.append((even, other))
    return sums, outgoing


def moved(sums, u, velocity, shear, bulk, load, step):
    even, other = sums
    v = [velocity[c] + step * (shear * even[c] + bulk * other[c] + load[c]) for c in range(3)]
    return v, [u[c] + step * v[c] for c in range(3)]


def prepare(sums, planes, velocity, shear, bulk, load, step, part_ref, up_ref, down_ref, rim_ref):
    sums, outgoing = sums
    last = len(planes) - 1
    for z, plane in enumerate(planes):
        v, displaced = moved(
            sums[z], plane.u, [velocity(c, z) for c in range(3)], shear(z), bulk(z),
            [load(c, z) for c in range(3)], step,
        )
        for c in range(3):
            part_ref[c, z] = v[c]
            for edge, ref in ((0, down_ref), (last, up_ref)):
                if z == edge:
                    ref[c] = plane.u[c]
                    ref[3 + c] = displaced[c]
    for c in range(6):
        rim_ref[0, c] = outgoing[0][c]
        rim_ref[1, c] = outgoing[last][c]


def zone_values(zone, shear_of, lame_of, zones, offset):
    shear = jnp.zeros(zone.shape, jnp.float32)
    bulk = jnp.zeros(zone.shape, jnp.float32)
    for k in range(zones):
        hit = zone == k + offset
        shear = jnp.where(hit, shear_of(k), shear)
        bulk = jnp.where(hit, shear_of(k) + lame_of(k), bulk)
    return shear, bulk


def open_kernel(
    step, state_hbm, load_hbm, zones_hbm, shear_hbm, lame_hbm, amp_hbm, cycle_hbm,
    moduli, loading, part, up, down, rim, zone_up, zone_down, zone_rows,
    state, load_shape, zones, shear_table, lame_table, amp_table, cycle_index, arrived,
):
    pairs = (
        (state_hbm.at[0, :3], state.at[:3]), (shear_hbm, shear_table), (lame_hbm, lame_table),
        (zones_hbm, zones), (cycle_hbm, cycle_index), (amp_hbm, amp_table),
        (load_hbm, load_shape), (state_hbm.at[0, 3:], state.at[3:]),
    )
    copies = [
        pltpu.make_async_copy(source, target, arrived.at[i])
        for i, (source, target) in enumerate(pairs)
    ]
    for copy in copies:
        copy.start()
    copies[0].wait()
    count, _, columns = zones.shape
    planes = [Inplane([state[c, z] for c in range(3)]) for z in range(count)]
    sums = own_sums(planes)
    for copy in copies[1:]:
        copy.wait()
    kinds = shear_table.shape[0]
    for z in range(count):
        moduli[0, z], moduli[1, z] = zone_values(
            zones[z], lambda k: shear_table[k], lambda k: lame_table[k], kinds, 0
        )
    amplitude = amp_table[cycle_index[lax.axis_index("win")]]
    for z in range(count):
        for c in range(3):
            loading[c, z] = amplitude * load_shape[c, z].astype(jnp.float32)
    prepare(
        sums, planes,
        lambda c, z: state[3 + c, z],
        lambda z: moduli[0, z],
        lambda z: moduli[1, z],
        lambda c, z: loading[c, z],
        step, part, up, down, rim,
    )
    zone_down[...] = (zones[0] + 1).astype(jnp.float32)
    zone_up[...] = (zones[count - 1] + 1).astype(jnp.float32)
    for k in range(kinds):
        zone_rows[k] = jnp.full((1, columns), shear_table[k], jnp.float32)
        zone_rows[kinds + k] = jnp.full((1, columns), lame_table[k], jnp.float32)


def two_steps(step, u0, part, rim, low, high, moduli, edges, load):
    count = moduli.shape[1]
    square = step * step
    sides = ((low, 0, 0, -1.0), (high, 1, count - 1, 1.0))
    velocities = [[part[c, z] for c in range(3)] for z in range(count)]
    outer = []
    for side, (got, edge, z, sign) in enumerate(sides):
        there = Inplane([got[c] for c in range(3)])
        even, odd = towards(sums_of(there), sign)
        for c in range(3):
            velocities[z][c] = velocities[z][c] + step * (
                moduli[0, z] * even[c] + moduli[1, z] * odd[c]
            )
        here = tuple(rim[side, c] for c in range(6)) + (u0[2, z],)
        even, odd = towards(here, -sign)
        outer.append(
            [
                got[3 + c] + square * (edges[2 * side] * even[c] + edges[2 * side + 1] * odd[c])
                for c in range(3)
            ]
        )
    planes = [
        Inplane([u0[c, z] + step * velocities[z][c] for c in range(3)]) for z in range(count)
    ]
    sums, _ = own_sums(planes)
    for side, (got, edge, z, sign) in enumerate(sides):
        part_of = towards(sums_of(Inplane(outer[side])), sign)
        sums[z] = tuple([a + b for a, b in zip(x, y)] for x, y in zip(sums[z], part_of))
    return [
        moved(
            sums[z], planes[z].u, velocities[z], moduli[0, z], moduli[1, z],
            [load(c, z) for c in range(3)], step,
        )
        for z in range(count)
    ]


def edge_kernel(zone_low, zone_high, zone_rows, up, down, edges, later_up, later_down):
    @pl.when(lax.axis_index("win") != 0)
    def _():
        kinds = zone_rows.shape[0] // 2
        for i, zone in enumerate((zone_low, zone_high)):
            edges[2 * i], edges[2 * i + 1] = zone_values(
                zone[...], lambda k: zone_rows[k], lambda k: zone_rows[kinds + k], kinds, 1.0
            )
        later_up[...] = up[...]
        later_down[...] = down[...]


def stored(state, ends):
    for z, (v, u) in enumerate(ends):
        for c in range(3):
            state[c, z] = u[c]
            state[3 + c, z] = v[c]


def fine_kernel(step, last, group, *refs):
    @pl.when((lax.axis_index("win") == 0) == (group == 0))
    def _():
        fine_pair(step, last, *refs)


def fine_pair(step, last, edges, state, moduli, loading, part, rim, low, high, *outs):
    load = lambda c, z: loading[c, z]
    ends = two_steps(step, state, part, rim, low, high, moduli, edges, load)
    stored(outs[0], ends)
    if not last:
        planes = [Inplane(u) for _, u in ends]
        prepare(
            own_sums(planes), planes, lambda c, z: ends[z][0][c], lambda z: moduli[0, z],
            lambda z: moduli[1, z], load, step, *outs[1:],
        )


def coarse_open_kernel(before, start, moduli, difference, part, up, down, rim):
    count = moduli.shape[1]
    planes = []
    for z in range(count):
        for c in range(6):
            difference[c, z] = before[c, z] - start[c, z]
        planes.append(Inplane([difference[c, z] for c in range(3)]))
    prepare(
        own_sums(planes), planes, lambda c, z: difference[3 + c, z], lambda z: moduli[0, z],
        lambda z: moduli[1, z], lambda c, z: 0.0, DT_COARSE, part, up, down, rim,
    )


def coarse_kernel(
    edges, state, moduli, part, rim, low, high, before_end, fine_end, new_end, end, left
):
    copies = [
        pltpu.make_async_copy(end.at[:, z], new_end.at[:, z], left.at[z])
        for z in range(moduli.shape[1])
    ]

    @pl.when(lax.axis_index("win") == 0)
    def _():
        end[...] = before_end[...]
        for copy in copies:
            copy.start()

    @pl.when(lax.axis_index("win") != 0)
    def _():
        ends = two_steps(
            DT_COARSE, state, part, rim, low, high, moduli, edges, lambda c, z: 0.0
        )
        for z, (v, u) in enumerate(ends):
            for c in range(3):
                end[c, z] = fine_end[c, z] + u[c]
                end[3 + c, z] = fine_end[3 + c, z] + v[c]
            copies[z].start()

    for copy in copies:
        copy.wait()


VMEM = pl.BlockSpec(memory_space=pltpu.VMEM)
HBM = pl.BlockSpec(memory_space=pltpu.HBM)


def called(kernel, outs, *operands, in_specs=None, out_specs=None, scratch=()):
    return pl.pallas_call(
        kernel,
        out_shape=[jax.ShapeDtypeStruct(shape, jnp.float32) for shape in outs],
        in_specs=in_specs or [VMEM] * len(operands),
        out_specs=out_specs or [VMEM] * len(outs),
        scratch_shapes=list(scratch),
        compiler_params=pltpu.CompilerParams(vmem_limit_bytes=16 * 1024 * 1024),
    )(*operands)


def exchanged(up, down, group):
    windows, slabs = lax.axis_size("win"), lax.axis_size("slab")

    def passed(block, distance):
        route = [
            (n * slabs + i - distance, n * slabs + i)
            for n in (range(1, windows) if group else range(1))
            for i in range(slabs)
            if 0 <= i - distance < slabs
        ]
        return lax.ppermute(block, ("win", "slab"), route)

    return passed(up, 1), passed(down, -1)


def in_hbm(*arrays):
    return [pltpu.with_memory_space_constraint(a, pltpu.HBM) for a in arrays]


def shards(states, load_shape, zone_ids, zone_shear, zone_lame, amp_table, cycle_index):
    windows = lax.axis_size("win")
    start = states[0]
    count, rows, columns = zone_ids.shape
    plane = (rows, columns)
    field, state = (3, count, *plane), (6, count, *plane)
    message, rims = (6, *plane), (2, 6, *plane)

    given = (states, load_shape, zone_ids, zone_shear, zone_lame, amp_table, cycle_index)
    tables = [pltpu.SMEM(table.shape, table.dtype) for table in given[3:]]
    zone_rows = (2 * zone_shear.shape[0], 1, columns)
    moduli, loading, part, up, down, rim, zone_up, zone_down, zone_rows = called(
        functools.partial(open_kernel, DT_FINE),
        [(2, count, *plane), field, field, message, message, rims, plane, plane, zone_rows],
        *in_hbm(*given),
        in_specs=[HBM] * len(given),
        scratch=[
            pltpu.VMEM(state, states.dtype),
            pltpu.VMEM(load_shape.shape, load_shape.dtype),
            pltpu.VMEM(zone_ids.shape, zone_ids.dtype),
            *tables,
            pltpu.SemaphoreType.DMA((len(given) + 1,)),
        ],
    )
    def fine(turn, group, *operands):
        last = turn == FINE // 2 - 1
        return called(
            functools.partial(fine_kernel, DT_FINE, last, group),
            [state] + ([] if last else [field, message, message, rims]),
            *operands,
        )

    after = lax.optimization_barrier
    fixed = moduli, loading
    low, high = exchanged(up, down, 0)
    edges, later_up, later_down = called(
        edge_kernel, [(4, *plane), message, message],
        *exchanged(zone_up, zone_down, 1), zone_rows, up, down,
    )
    edges = lax.ppermute(
        edges, "win", [(0, 1), (1, 0)] + [(n, n) for n in range(2, windows)]
    ), edges
    later_low, later_high = exchanged(later_up, later_down, 1)
    ends, parts, rim_of = [start, start], [part, part], [rim, rim]
    for turn in range(FINE // 2):
        last = turn == FINE // 2 - 1
        got = [(low, high), (later_low, later_high)]
        for group in (0, 1):
            if group == 0 or not last:
                ends[group], *more = fine(
                    turn, group, edges[group], ends[group], *fixed, parts[group], rim_of[group],
                    *got[group],
                )
                if not last:
                    parts[group], up, down, rim_of[group] = more
                    if group == 0:
                        low, high = exchanged(up, down, 0)
                        later_low, later_high, _ = after((later_low, later_high, parts[0]))
                        got[1] = later_low, later_high
                    else:
                        later_low, later_high = exchanged(up, down, 1)
                        low, high, _ = after((low, high, parts[1]))

    new_end = ends[0]
    for link in range(windows - 1):
        before = lax.ppermute(new_end, "win", [(n, n + 1) for n in range(windows - 1)])
        difference, part, up, down, rim = called(
            coarse_open_kernel, [state, field, message, message, rims], before, start, moduli
        )
        low, high = exchanged(up, down, 1)
        if link == 0:
            later_low, later_high, _ = after((later_low, later_high, part))
            fine_end = fine(
                FINE // 2 - 1, 1, edges[1], ends[1], *fixed, parts[1], rim_of[1],
                later_low, later_high,
            )[0]
        new_end = called(
            coarse_kernel, [state],
            edges[1], difference, moduli, part, rim, low, high, ends[0], fine_end,
            out_specs=[HBM],
            scratch=[pltpu.VMEM(state, jnp.float32), pltpu.SemaphoreType.DMA((count,))],
        )[0]
    return new_end[None]


def solution(mesh):
    placed = (
        P("win", None, "slab", None, None),
        P(None, "slab", None, None),
        P("slab", None, None),
        P(),
        P(),
        P(),
        P(),
    )

    return jax.shard_map(
        shards,
        mesh=mesh,
        in_specs=placed,
        out_specs=P("win", None, "slab", None, None),
        check_vma=False,
    )
```

```python
import functools

import jax
import jax.numpy as jnp
from jax import lax
from jax.experimental import pallas as pl
from jax.experimental.pallas import tpu as pltpu
from jax.sharding import PartitionSpec as P

FINE = 4
DT_FINE = 0.18
DT_COARSE = 0.36


class Inplane:
    def __init__(self, u):
        rows, columns = u[0].shape
        tile, lanes = 8, columns // 2
        row = lax.broadcasted_iota(jnp.int32, (tile, columns), 0)
        lane = lax.broadcasted_iota(jnp.int32, (rows, lanes), 1)

        def shifted(f, axis, up):
            turned = pltpu.roll(f, f.shape[axis] - 1 if up else 1, axis)
            if axis == 0 and up:
                edge = jnp.where(row == tile - 1, 0.0, turned[rows - tile :])
                return jnp.concatenate([turned[: rows - tile], edge], axis=0)
            if axis == 0:
                edge = jnp.where(row == 0, 0.0, turned[:tile])
                return jnp.concatenate([edge, turned[tile:]], axis=0)
            if up:
                edge = jnp.where(lane == lanes - 1, 0.0, turned[:, lanes:])
                return jnp.concatenate([turned[:, :lanes], edge], axis=1)
            edge = jnp.where(lane == 0, 0.0, turned[:, :lanes])
            return jnp.concatenate([edge, turned[:, lanes:]], axis=1)

        self.u = u
        self.shifted = shifted
        plus = [shifted(f, 1, True) for f in u]
        minus = [shifted(f, 1, False) for f in u]
        self.sum_x = [a + b for a, b in zip(plus, minus)]
        self.diff_x = [a - b for a, b in zip(plus, minus)]
        self.up_y = [None, shifted(u[1], 0, True), shifted(u[2], 0, True)]
        self.down_y = [None, shifted(u[1], 0, False), shifted(u[2], 0, False)]
        self.even = []
        for f, s in zip(u, self.sum_x):
            across = s + 3.0 * f
            square = shifted(across, 0, True) + shifted(across, 0, False) + 3.0 * across
            self.even.append((square + 5.0 * f) * (1.0 / 30.0))
        self.odd = [
            0.25 * self.diff_x[2],
            0.25 * (self.up_y[2] - self.down_y[2]),
            0.25 * (self.diff_x[0] + (self.up_y[1] - self.down_y[1])),
        ]

    def own(self):
        u, shifted = self.u, self.shifted
        up_x, down_x = shifted(u[0], 0, True), shifted(u[0], 0, False)
        sum_y = [up_x + down_x, self.up_y[1] + self.down_y[1], self.up_y[2] + self.down_y[2]]
        shear = [
            3.0 * e + (s + t) * (1.0 / 6.0) - (17.0 / 3.0) * f
            for e, s, t, f in zip(self.even, self.sum_x, sum_y, u)
        ]
        cross = [
            0.25 * (shifted(d, 0, True) - shifted(d, 0, False)) for d in self.diff_x[:2]
        ]
        bulk = [
            self.sum_x[0] - 2.0 * u[0] + cross[1],
            sum_y[1] - 2.0 * u[1] + cross[0],
            -2.0 * u[2],
        ]
        return shear, bulk


def towards(plane_sums, sign):
    odd = [sign * f for f in plane_sums[3:6]]
    return plane_sums[:3], [odd[0], odd[1], odd[2] + plane_sums[6]]


def sums_of(inplane):
    return (*inplane.even, *inplane.odd, inplane.u[2])


def own_sums(planes):
    count = len(planes)
    outgoing = [sums_of(p) for p in planes]
    sums = []
    for z, plane in enumerate(planes):
        even, other = plane.own()
        for neighbour, sign in ((z - 1, -1.0), (z + 1, 1.0)):
            if 0 <= neighbour < count:
                e, o = towards(outgoing[neighbour], sign)
                even = [a + b for a, b in zip(even, e)]
                other = [a + b for a, b in zip(other, o)]
        sums.append((even, other))
    return sums, outgoing


def moved(sums, u, velocity, shear, bulk, load, step):
    even, other = sums
    v = [velocity[c] + step * (shear * even[c] + bulk * other[c] + load[c]) for c in range(3)]
    return v, [u[c] + step * v[c] for c in range(3)]


def prepare(sums, planes, velocity, shear, bulk, load, step, part_ref, up_ref, down_ref, rim_ref):
    sums, outgoing = sums
    last = len(planes) - 1
    for z, plane in enumerate(planes):
        v, displaced = moved(
            sums[z], plane.u, [velocity(c, z) for c in range(3)], shear(z), bulk(z),
            [load(c, z) for c in range(3)], step,
        )
        for c in range(3):
            part_ref[c, z] = v[c]
            for edge, ref in ((0, down_ref), (last, up_ref)):
                if z == edge:
                    ref[c] = plane.u[c]
                    ref[3 + c] = displaced[c]
    for c in range(6):
        rim_ref[0, c] = outgoing[0][c]
        rim_ref[1, c] = outgoing[last][c]


def zone_values(zone, shear_of, lame_of, zones, offset):
    shear = jnp.zeros(zone.shape, jnp.float32)
    bulk = jnp.zeros(zone.shape, jnp.float32)
    for k in range(zones):
        hit = zone == k + offset
        shear = jnp.where(hit, shear_of(k), shear)
        bulk = jnp.where(hit, shear_of(k) + lame_of(k), bulk)
    return shear, bulk


def open_kernel(
    step, state_hbm, load_hbm, zones_hbm, shear_hbm, lame_hbm, amp_hbm, cycle_hbm,
    moduli, loading, part, up, down, rim, zone_up, zone_down, zone_rows,
    state, load_shape, zones, shear_table, lame_table, amp_table, cycle_index, arrived,
):
    pairs = (
        (state_hbm.at[0, :3], state.at[:3]), (shear_hbm, shear_table), (lame_hbm, lame_table),
        (zones_hbm, zones), (cycle_hbm, cycle_index), (amp_hbm, amp_table),
        (load_hbm, load_shape), (state_hbm.at[0, 3:], state.at[3:]),
    )
    copies = [
        pltpu.make_async_copy(source, target, arrived.at[i])
        for i, (source, target) in enumerate(pairs)
    ]
    for copy in copies:
        copy.start()
    copies[0].wait()
    count, _, columns = zones.shape
    planes = [Inplane([state[c, z] for c in range(3)]) for z in range(count)]
    sums = own_sums(planes)
    for copy in copies[1:]:
        copy.wait()
    kinds = shear_table.shape[0]
    for z in range(count):
        moduli[0, z], moduli[1, z] = zone_values(
            zones[z], lambda k: shear_table[k], lambda k: lame_table[k], kinds, 0
        )
    amplitude = amp_table[cycle_index[lax.axis_index("win")]]
    for z in range(count):
        for c in range(3):
            loading[c, z] = amplitude * load_shape[c, z].astype(jnp.float32)
    prepare(
        sums, planes,
        lambda c, z: state[3 + c, z],
        lambda z: moduli[0, z],
        lambda z: moduli[1, z],
        lambda c, z: loading[c, z],
        step, part, up, down, rim,
    )
    zone_down[...] = (zones[0] + 1).astype(jnp.float32)
    zone_up[...] = (zones[count - 1] + 1).astype(jnp.float32)
    for k in range(kinds):
        zone_rows[k] = jnp.full((1, columns), shear_table[k], jnp.float32)
        zone_rows[kinds + k] = jnp.full((1, columns), lame_table[k], jnp.float32)


def side_sums(step, got, here, shear, bulk, edge_shear, edge_bulk, sign):
    there = Inplane([got[c] for c in range(3)])
    even, odd = towards(sums_of(there), sign)
    velocity = [step * (shear * even[c] + bulk * odd[c]) for c in range(3)]
    even, odd = towards(here, -sign)
    square = step * step
    outer = [
        got[3 + c] + square * (edge_shear * even[c] + edge_bulk * odd[c]) for c in range(3)
    ]
    return velocity, towards(sums_of(Inplane(outer)), sign)


def slab_side(step, side, u0, rim, got, moduli, edges):
    z, sign = ((0, -1.0), (moduli.shape[1] - 1, 1.0))[side]
    here = tuple(rim[side, c] for c in range(6)) + (u0[2, z],)
    return side_sums(
        step, got, here, moduli[0, z], moduli[1, z], edges[2 * side], edges[2 * side + 1], sign
    )


def share_kernel(step, side, edges, u0, moduli, rim, got, share):
    @pl.when(lax.axis_index("win") != 0)
    def _():
        velocity, (even, odd) = slab_side(step, side, u0, rim, got, moduli, edges)
        for c in range(3):
            share[c], share[3 + c], share[6 + c] = velocity[c], even[c], odd[c]


def two_steps(step, u0, part, rim, low, high, moduli, edges, load, shared=None):
    count = moduli.shape[1]
    velocities = [[part[c, z] for c in range(3)] for z in range(count)]
    sides = []
    for side, got in enumerate((low, high)):
        if side == shared:
            velocity, even, odd = ([got[first + c] for c in range(3)] for first in (0, 3, 6))
            sides.append((velocity, (even, odd)))
        else:
            sides.append(slab_side(step, side, u0, rim, got, moduli, edges))
    edge_planes = (0, count - 1)
    for z, (velocity, _) in zip(edge_planes, sides):
        velocities[z] = [a + b for a, b in zip(velocities[z], velocity)]
    planes = [
        Inplane([u0[c, z] + step * velocities[z][c] for c in range(3)]) for z in range(count)
    ]
    sums, _ = own_sums(planes)
    for z, (_, side) in zip(edge_planes, sides):
        sums[z] = tuple([a + b for a, b in zip(x, y)] for x, y in zip(sums[z], side))
    return [
        moved(
            sums[z], planes[z].u, velocities[z], moduli[0, z], moduli[1, z],
            [load(c, z) for c in range(3)], step,
        )
        for z in range(count)
    ]


def edge_kernel(zone_low, zone_high, zone_rows, up, down, edges, later_up, later_down):
    @pl.when(lax.axis_index("win") != 0)
    def _():
        kinds = zone_rows.shape[0] // 2
        for i, zone in enumerate((zone_low, zone_high)):
            edges[2 * i], edges[2 * i + 1] = zone_values(
                zone[...], lambda k: zone_rows[k], lambda k: zone_rows[kinds + k], kinds, 1.0
            )
        later_up[...] = up[...]
        later_down[...] = down[...]


def stored(state, ends):
    for z, (v, u) in enumerate(ends):
        for c in range(3):
            state[c, z] = u[c]
            state[3 + c, z] = v[c]


def fine_kernel(step, last, group, *refs):
    @pl.when((lax.axis_index("win") == 0) == (group == 0))
    def _():
        fine_pair(step, last, *refs)


def fine_pair(step, last, edges, state, moduli, loading, part, rim, low, high, *outs):
    load = lambda c, z: loading[c, z]
    ends = two_steps(step, state, part, rim, low, high, moduli, edges, load)
    stored(outs[0], ends)
    if not last:
        planes = [Inplane(u) for _, u in ends]
        prepare(
            own_sums(planes), planes, lambda c, z: ends[z][0][c], lambda z: moduli[0, z],
            lambda z: moduli[1, z], load, step, *outs[1:],
        )


def coarse_open_kernel(before, start, moduli, difference, part, up, down, rim):
    count = moduli.shape[1]
    planes = []
    for z in range(count):
        for c in range(6):
            difference[c, z] = before[c, z] - start[c, z]
        planes.append(Inplane([difference[c, z] for c in range(3)]))
    prepare(
        own_sums(planes), planes, lambda c, z: difference[3 + c, z], lambda z: moduli[0, z],
        lambda z: moduli[1, z], lambda c, z: 0.0, DT_COARSE, part, up, down, rim,
    )


def coarse_kernel(
    edges, state, moduli, part, rim, low, high, before_end, fine_end, new_end, end, left
):
    copies = [
        pltpu.make_async_copy(end.at[:, z], new_end.at[:, z], left.at[z])
        for z in range(moduli.shape[1])
    ]

    @pl.when(lax.axis_index("win") == 0)
    def _():
        end[...] = before_end[...]
        for copy in copies:
            copy.start()

    @pl.when(lax.axis_index("win") != 0)
    def _():
        ends = two_steps(
            DT_COARSE, state, part, rim, low, high, moduli, edges, lambda c, z: 0.0, 0
        )
        for z, (v, u) in enumerate(ends):
            for c in range(3):
                end[c, z] = fine_end[c, z] + u[c]
                end[3 + c, z] = fine_end[3 + c, z] + v[c]
            copies[z].start()

    for copy in copies:
        copy.wait()


VMEM = pl.BlockSpec(memory_space=pltpu.VMEM)
HBM = pl.BlockSpec(memory_space=pltpu.HBM)


def called(kernel, outs, *operands, in_specs=None, out_specs=None, scratch=()):
    return pl.pallas_call(
        kernel,
        out_shape=[jax.ShapeDtypeStruct(shape, jnp.float32) for shape in outs],
        in_specs=in_specs or [VMEM] * len(operands),
        out_specs=out_specs or [VMEM] * len(outs),
        scratch_shapes=list(scratch),
        compiler_params=pltpu.CompilerParams(vmem_limit_bytes=16 * 1024 * 1024),
    )(*operands)


def exchanged(up, down, group):
    windows, slabs = lax.axis_size("win"), lax.axis_size("slab")

    def passed(block, distance):
        route = [
            (n * slabs + i - distance, n * slabs + i)
            for n in (range(1, windows) if group else range(1))
            for i in range(slabs)
            if 0 <= i - distance < slabs
        ]
        return lax.ppermute(block, ("win", "slab"), route)

    return passed(up, 1), passed(down, -1)


def in_hbm(*arrays):
    return [pltpu.with_memory_space_constraint(a, pltpu.HBM) for a in arrays]


def shards(states, load_shape, zone_ids, zone_shear, zone_lame, amp_table, cycle_index):
    windows = lax.axis_size("win")
    start = states[0]
    count, rows, columns = zone_ids.shape
    plane = (rows, columns)
    field, state = (3, count, *plane), (6, count, *plane)
    message, rims = (6, *plane), (2, 6, *plane)

    given = (states, load_shape, zone_ids, zone_shear, zone_lame, amp_table, cycle_index)
    tables = [pltpu.SMEM(table.shape, table.dtype) for table in given[3:]]
    zone_rows = (2 * zone_shear.shape[0], 1, columns)
    moduli, loading, part, up, down, rim, zone_up, zone_down, zone_rows = called(
        functools.partial(open_kernel, DT_FINE),
        [(2, count, *plane), field, field, message, message, rims, plane, plane, zone_rows],
        *in_hbm(*given),
        in_specs=[HBM] * len(given),
        scratch=[
            pltpu.VMEM(state, states.dtype),
            pltpu.VMEM(load_shape.shape, load_shape.dtype),
            pltpu.VMEM(zone_ids.shape, zone_ids.dtype),
            *tables,
            pltpu.SemaphoreType.DMA((len(given) + 1,)),
        ],
    )
    def fine(turn, group, *operands):
        last = turn == FINE // 2 - 1
        return called(
            functools.partial(fine_kernel, DT_FINE, last, group),
            [state] + ([] if last else [field, message, message, rims]),
            *operands,
        )

    after = lax.optimization_barrier
    fixed = moduli, loading
    low, high = exchanged(up, down, 0)
    edges, later_up, later_down = called(
        edge_kernel, [(4, *plane), message, message],
        *exchanged(zone_up, zone_down, 1), zone_rows, up, down,
    )
    edges = lax.ppermute(
        edges, "win", [(0, 1), (1, 0)] + [(n, n) for n in range(2, windows)]
    ), edges
    later_low, later_high = exchanged(later_up, later_down, 1)
    ends, parts, rim_of = [start, start], [part, part], [rim, rim]
    for turn in range(FINE // 2):
        last = turn == FINE // 2 - 1
        got = [(low, high), (later_low, later_high)]
        for group in (0, 1):
            if group == 0 or not last:
                ends[group], *more = fine(
                    turn, group, edges[group], ends[group], *fixed, parts[group], rim_of[group],
                    *got[group],
                )
                if not last:
                    parts[group], up, down, rim_of[group] = more
                    if group == 0:
                        low, high = exchanged(up, down, 0)
                        later_low, later_high, _ = after((later_low, later_high, parts[0]))
                        got[1] = later_low, later_high
                    else:
                        later_low, later_high = exchanged(up, down, 1)
                        low, high, _ = after((low, high, parts[1]))

    new_end = ends[0]
    for link in range(windows - 1):
        before = lax.ppermute(new_end, "win", [(n, n + 1) for n in range(windows - 1)])
        difference, part, up, down, rim = called(
            coarse_open_kernel, [state, field, message, message, rims], before, start, moduli
        )
        low, high = exchanged(up, down, 1)
        if link == 0:
            later_low, later_high, _ = after((later_low, later_high, part))
            fine_end = fine(
                FINE // 2 - 1, 1, edges[1], ends[1], *fixed, parts[1], rim_of[1],
                later_low, later_high,
            )[0]
        share = called(
            functools.partial(share_kernel, DT_COARSE, 0), [(9, *plane)],
            edges[1], difference, moduli, rim, low,
        )[0]
        new_end = called(
            coarse_kernel, [state],
            edges[1], difference, moduli, part, rim, share, high, ends[0], fine_end,
            out_specs=[HBM],
            scratch=[pltpu.VMEM(state, jnp.float32), pltpu.SemaphoreType.DMA((count,))],
        )[0]
    return new_end[None]


def solution(mesh):
    placed = (
        P("win", None, "slab", None, None),
        P(None, "slab", None, None),
        P("slab", None, None),
        P(),
        P(),
        P(),
        P(),
    )

    return jax.shard_map(
        shards,
        mesh=mesh,
        in_specs=placed,
        out_specs=P("win", None, "slab", None, None),
        check_vma=False,
    )
```
